512 devices in a mesh: row: 16 (over z, core), col: 16 (over y, x_hi), seed: 2 (over x_lo).
Axes of the slice: x: 4 (x_hi: 2, x_lo: 2; x = x_hi * 2 + x_lo), y: 8, z: 8, core: 2. Of those that a mesh axis runs over, the one named last changes fastest.
Arguments:
- tokens_act: float32 [4096, 768], P(('seed', 'row')), parts along dimension 0, may hold values from -6 to 6
- single_cond: float32 [4096, 384], P(('seed', 'row')), parts along dimension 0, may hold values from -6 to 6
- noise_level: float32 [2], P('seed'), parts along dimension 0, may hold values from 0.04 to 160
- fourier_freq: float32 [256], replicated, may hold values from -4 to 4
- fourier_phase: float32 [256], replicated, may hold values from 0 to 1
- noise_weight: float32 [256, 384], replicated, may hold values from -0.375 to 0.375
- ada_weight: float32 [384, 1536], replicated, may hold values from -0.3125 to 0.3125
- query_gate_weight: float32 [768, 1536], replicated, may hold values from -0.21875 to 0.21875
- kv_weight: float32 [768, 1536], replicated, may hold values from -0.21875 to 0.21875
- out_weight: float32 [768, 768], replicated, may hold values from -0.21875 to 0.21875
- out_gate_weight: float32 [384, 768], replicated, may hold values from -0.3125 to 0.3125
- pair_bias: bfloat16 [16, 2048, 2048], P(None, 'row', 'col'), may hold values from -384 to 384
- relpos_table: float32 [16, 66], replicated, may hold values from -5 to 5
- chain_id: int32 [2048], replicated, may hold values from 0 to 7, never falling along the last dimension, each value on 1 to 1024 neighbouring positions
- residue_index: int32 [2048], replicated, may hold values from 0 to 3071, as said below
Outputs:
- updated: float32 [4096, 768], P(('seed', 'row')), parts along dimension 0
The draws below stay inside these ranges and needn't reach their ends.
There are 2 independent parts, one for each index of `seed`. The reference program is written for one: setup_inputs(seed, part) draws one part's arguments, and reference() takes and returns one part's arrays. A program takes and returns all parts, laid end to end along the dimension named above; an argument that names none is the same for every part. Nothing has to cross between parts.
Inputs may be any that keep to these rules, and one draw needn't show every extreme that they name: `residue_index`: the first token's residue number is 0; residue numbers never fall along the tokens and rise by 1 or 2 from one token to the next. `chain_id`: chain numbers never fall along the tokens.
All inputs are finite; a program needn't handle non-finite values.
Results may differ from the reference program's by a relative error of at most 0.0003.
Values sent between devices are 32-bit elements; how exact they have to be, the bound alone decides.
A program may use at most 64 MiB of HBM per device.

```python
import math
import jax
import jax.numpy as jnp
import numpy as np
from jax import lax

D = 768
HEADS = 16
HEAD_DIM = 48
C_S = 384
FOURIER = 256
REL = 32
CHAINS = 8
TOK_DEV = 128
TOKENS = 2048
N_ROW = 16


def draw_pair_bias(key, part):
    key = jax.random.fold_in(key, 5)
    keys_split = jax.random.split(key, 1)
    base = jax.random.normal(keys_split[0], (HEADS, TOKENS, TOKENS), jnp.float32)
    return base.astype(jnp.bfloat16)


def draw_residue_index(key, part):
    key = jax.random.fold_in(key, 11)
    order = jax.random.permutation(key, TOKENS - 1)
    steps = jnp.where(order < TOKENS // 2, 2, 1).astype(jnp.int32)
    running = jnp.cumsum(steps).astype(jnp.int32)
    return jnp.concatenate([jnp.zeros((1,), jnp.int32), running]).astype(jnp.int32)


def block_scale(own_key, dims, pieces, low, largest):
    gain, own = 1.0, jax.random.fold_in(own_key, 6)
    for dim, blocks in pieces:
        draws = jnp.exp(jax.random.uniform(jax.random.fold_in(own, dim), (blocks,), jnp.float32, low / len(pieces), largest / len(pieces)))
        gain = gain * jnp.repeat(draws, dims[dim] // blocks).reshape([-1 if axis == dim else 1 for axis in range(len(dims))])
    return gain


def split_up(amount, total, most, skew):
    portions = [(1 << 20) // math.isqrt(grade ** skew) + 1 for grade in range(2, amount + 1)]
    surplus, given = total - most - (amount - 1), [1] * (amount - 1)
    while surplus > 0:
        movable = [i for i in range(amount - 1) if given[i] < most]
        whole, left = sum([portions[i] for i in movable]), surplus
        for i in movable:
            more = min(most - given[i], max(1, left * portions[i] // whole), surplus)
            given[i] = given[i] + more
            surplus = surplus - more
    return np.array([most] + given)


def ragged(key, amount, total, reach, skew):
    if amount == 2:
        one = jax.random.randint(key, (), max(1, total - reach), min(reach, total - 1) + 1)
        return jnp.stack([one, total - one])
    tallies = jnp.asarray(split_up(amount, total, reach, skew), jnp.int32)
    twos = (amount - 1) // 2
    donor, sink = tallies[1:1 + 2 * twos:2], tallies[2:2 + 2 * twos:2]
    room = jnp.minimum(donor - 1, reach - sink)
    moved = jax.random.randint(jax.random.fold_in(key, 1), (twos,), 0, 1 << 20) % (room + 1)
    tallies = tallies.at[1:1 + 2 * twos:2].set(donor - moved).at[2:2 + 2 * twos:2].set(sink + moved)
    return tallies[jax.random.permutation(jax.random.fold_in(key, 2), amount)]


def bell_draw(own_key, shape, spread, most, cuts=(), kind=jnp.bfloat16):
    level = block_scale(own_key, shape, cuts, -0.22, 0.18) if cuts else 1.0
    drawn = jax.random.normal(own_key, shape, jnp.float32) * spread * level
    return jnp.minimum(jnp.maximum(drawn, -most), most).astype(kind)


def setup_inputs(seed: int = 0, part: int = 0) -> dict:
    seeds = jax.random.split(jax.random.key(seed), 16)
    part_keys = jax.random.split(jax.random.fold_in(seeds[15], part), 16)
    return {
        "tokens_act": bell_draw(part_keys[0], (TOKENS, D), 1.0, 6.0, ((0, 16),), jnp.float32),
        "single_cond": bell_draw(part_keys[1], (TOKENS, C_S), 1.0, 6.0, ((0, 16),), jnp.float32),
        "noise_level": jnp.clip(jnp.exp(jax.random.uniform(part_keys[2], (1,), jnp.float32, math.log(0.04), math.log(160.0))), 0.04, 160.0),
        "fourier_freq": bell_draw(seeds[3], (FOURIER,), 1.0, 4.0, (), jnp.float32),
        "fourier_phase": jnp.clip(jax.random.uniform(seeds[4], (FOURIER,), jnp.float32, 0.0, 1.0), 0.0, 1.0),
        "noise_weight": bell_draw(seeds[5], (FOURIER, C_S), FOURIER ** -0.5, 0.375, (), jnp.float32),
        "ada_weight": bell_draw(seeds[6], (C_S, 2 * D), C_S ** -0.5, 0.3125, (), jnp.float32),
        "query_gate_weight": bell_draw(seeds[7], (D, 2 * D), D ** -0.5, 0.21875, (), jnp.float32),
        "kv_weight": bell_draw(seeds[8], (D, 2 * D), D ** -0.5, 0.21875, (), jnp.float32),
        "out_weight": bell_draw(seeds[9], (D, D), D ** -0.5, 0.21875, (), jnp.float32),
        "out_gate_weight": bell_draw(seeds[10], (C_S, D), C_S ** -0.5, 0.3125, (), jnp.float32),
        "pair_bias": draw_pair_bias(jax.random.fold_in(seeds[15], 71), part),
        "relpos_table": bell_draw(seeds[12], (HEADS, 2 * REL + 2), 1.0, 5.0, (), jnp.float32),
        "chain_id": jnp.searchsorted(jnp.cumsum(ragged(seeds[13], CHAINS, TOKENS, TOKENS // 2, 1)), jnp.arange(TOKENS), side="right").astype(jnp.int32),
        "residue_index": draw_residue_index(jax.random.fold_in(seeds[15], 71), part),
    }


def layer_norm(inputs):
    average = lax.optimization_barrier(jnp.mean(inputs, axis=-1, keepdims=True))
    centred = inputs - average
    variance = lax.optimization_barrier(jnp.mean(centred * centred, axis=-1, keepdims=True))
    return centred * lax.rsqrt(variance + 1e-05)

def matmul_high(left, right):
    return jnp.dot(left, right, precision=lax.Precision.HIGHEST, preferred_element_type=jnp.float32)

def relative_bias(relpos_table, chain_query, chain_key, residue_query, residue_key):
    query_count = chain_query.shape[0]
    block_rows = math.gcd(query_count, 64)
    classes = jnp.arange(2 * REL + 2, dtype=jnp.int32)

    def one_block(block_index):
        start = (block_index * block_rows).astype(jnp.int32)
        chain_part = lax.dynamic_slice_in_dim(chain_query, start, block_rows, 0)
        residue_part = lax.dynamic_slice_in_dim(residue_query, start, block_rows, 0)
        offset = jnp.clip(residue_part[:, None] - residue_key[None, :], -REL, REL) + REL
        bucket = jnp.where(chain_part[:, None] == chain_key[None, :], offset, 2 * REL + 1).astype(jnp.int32)
        onehot = (bucket[None, :, :] == classes[:, None, None]).astype(jnp.float32)
        return jnp.einsum('hc,cqk->hqk', relpos_table, onehot, precision=lax.Precision.HIGHEST)
    blocks = lax.map(one_block, jnp.arange(query_count // block_rows, dtype=jnp.int32))
    return jnp.transpose(blocks, (1, 0, 2, 3)).reshape(relpos_table.shape[0], query_count, chain_key.shape[0])

def reference(tokens_act, single_cond, noise_level, fourier_freq, fourier_phase, noise_weight, ada_weight, query_gate_weight, kv_weight, out_weight, out_gate_weight, pair_bias, relpos_table, chain_id, residue_index):
    noise_scaled = 0.25 * jnp.log(noise_level[0] / 16.0)
    features = jnp.cos(2.0 * jnp.pi * (noise_scaled * fourier_freq + fourier_phase))
    cond_norm = layer_norm(single_cond + matmul_high(layer_norm(features)[None, :], noise_weight))
    ada_terms = matmul_high(cond_norm, ada_weight)
    modulated = jax.nn.sigmoid(ada_terms[:, :D]) * layer_norm(tokens_act) + ada_terms[:, D:]
    query_gate = matmul_high(modulated, query_gate_weight)
    key_value = matmul_high(modulated, kv_weight)
    keys = key_value[:, :D].reshape(TOKENS, HEADS, HEAD_DIM)
    values = key_value[:, D:].reshape(TOKENS, HEADS, HEAD_DIM)
    score_scale = 1.0 / jnp.sqrt(jnp.float32(HEAD_DIM))

    def attend_block(block_index):
        offset = (block_index * TOK_DEV).astype(jnp.int32)
        queries = lax.dynamic_slice_in_dim(query_gate[:, :D], offset, TOK_DEV, 0).reshape(TOK_DEV, HEADS, HEAD_DIM)
        bias_rows = lax.dynamic_slice_in_dim(pair_bias, offset, TOK_DEV, 1).astype(jnp.float32)
        relpos = relative_bias(relpos_table, lax.dynamic_slice_in_dim(chain_id, offset, TOK_DEV, 0), chain_id, lax.dynamic_slice_in_dim(residue_index, offset, TOK_DEV, 0), residue_index)
        scores = jnp.einsum('qhd,khd->hqk', queries, keys, precision=lax.Precision.HIGHEST) * score_scale + bias_rows + relpos
        weights = jax.nn.softmax(scores, axis=2)
        return jnp.einsum('hqk,khd->qhd', weights, values, precision=lax.Precision.HIGHEST).reshape(TOK_DEV, D)
    attended = lax.map(attend_block, jnp.arange(N_ROW, dtype=jnp.int32)).reshape(TOKENS, D)
    gated = jax.nn.sigmoid(query_gate[:, D:]) * attended
    update = jax.nn.sigmoid(matmul_high(cond_norm, out_gate_weight)) * matmul_high(gated, out_weight)
    return tokens_act + update
```

```python
import jax
import jax.numpy as jnp
from jax import lax
from jax.experimental import pallas as pl
from jax.experimental.pallas import tpu as pltpu
from jax.sharding import PartitionSpec as P

D = 768
HEADS = 16
HEAD_DIM = 48
C_S = 384
REL = 32
TOK = 128
N_ROW = 16
N_COL = 16
SLICES = 8
SLICE_ROWS = TOK // SLICES
MSG_ROWS = 56
MESH = pl.DeviceIdType.MESH
F32 = jnp.float32
BF16 = jnp.bfloat16


def split(value):
    high = value.astype(BF16)
    low = (value - high.astype(F32)).astype(BF16)
    return high, low


def mul(left, right):
    return jnp.dot(left, right, preferred_element_type=F32)


def stacked(value):
    high, low = split(value)
    return jnp.concatenate([high, low], axis=0)


def dot_split(both, right_high, right_low):
    rows = both.shape[0] // 2
    first = mul(both, right_high)
    return first[:rows] + first[rows:] + mul(both[:rows], right_low)


def layer_norm(inputs):
    average = jnp.mean(inputs, axis=-1, keepdims=True)
    centred = inputs - average
    variance = jnp.mean(centred * centred, axis=-1, keepdims=True)
    return centred * lax.rsqrt(variance + 1e-05)


def sigmoid(value):
    return 1.0 / (1.0 + jnp.exp(-value))


def kernel(
    tokens_hbm,
    cond_hbm,
    noise_ref,
    freq_hbm,
    phase_hbm,
    noise_w_hbm,
    ada_w_hbm,
    qg_w_hbm,
    kv_w_hbm,
    out_w_hbm,
    og_w_hbm,
    bias_hbm,
    table_hbm,
    chain_hbm,
    residue_hbm,
    out_ref,
    tokens,
    cond,
    freq,
    phase,
    noise_w,
    ada_w,
    qg_w,
    kv_w,
    out_w,
    og_w,
    bias,
    table,
    chain,
    residue,
    ada,
    modulated,
    block,
    q_high,
    q_low,
    gates,
    out_gate,
    q_t,
    v_t,
    k_high,
    k_low,
    kv_high,
    kv_low,
    scores_bias,
    parts_out,
    parts_in,
    attended,
    load_sems,
    block_send,
    block_recv,
    mate_send,
    mate_recv,
    part_send,
    part_recv,
    att_send,
    att_recv,
):
    row = lax.axis_index("row")
    col = lax.axis_index("col")
    seed = lax.axis_index("seed")
    core = lax.rem(row, 2)
    col_y, col_x = col // 2, lax.rem(col, 2)
    mate = (row + 1 - 2 * core, col, seed)
    is_source = core == col_x

    pairs = (
        (cond_hbm, cond),
        (freq_hbm, freq),
        (phase_hbm, phase),
        (noise_w_hbm, noise_w),
        (ada_w_hbm, ada_w),
        (tokens_hbm, tokens),
        (qg_w_hbm, qg_w),
        (chain_hbm, chain),
        (residue_hbm, residue),
        (table_hbm, table),
        (bias_hbm, bias),
        (og_w_hbm, og_w),
        (kv_w_hbm, kv_w),
        (out_w_hbm, out_w),
    )
    loads = {}
    for number, (source, target) in enumerate(pairs):
        copy = pltpu.make_async_copy(source, target, load_sems.at[number])
        copy.start()
        loads[number] = copy

    barrier = pltpu.get_barrier_semaphore()

    def greet(step, _):
        pl.semaphore_signal(
            barrier,
            inc=1,
            device_id=(row, lax.rem(col + step, N_COL), seed),
            device_id_type=MESH,
        )
        return 0

    def greet_source(step, _):
        source_col = 2 * (2 * step + core) + lax.rem(col, 2)

        @pl.when(jnp.logical_not((row == col) & (source_col == col)))
        def _():
            pl.semaphore_signal(
                barrier, inc=1, device_id=(col, source_col, seed), device_id_type=MESH
            )

        return 0

    lax.fori_loop(0, SLICES // 2, greet_source, 0)
    lax.fori_loop(1, N_COL, greet, 0)
    pl.semaphore_signal(barrier, inc=1, device_id=mate, device_id_type=MESH)
    to_self = (row == col) & (lax.rem(col_y, 2) == core)
    expected = (
        N_COL - 1 + 1 + jnp.where(is_source, SLICES, 0) - jnp.where(to_self, 1, 0)
    )

    for number in (0, 1, 2, 3):
        loads[number].wait()
    level = jnp.full((2, 128), noise_ref[0, 0], F32)
    noise_scaled = 0.25 * jnp.log(level / 16.0)
    features = jnp.cos(2.0 * jnp.pi * (noise_scaled * freq[...] + phase[...]))
    average = jnp.sum(features, keepdims=True) / 256.0
    centred = features - average
    variance = jnp.sum(centred * centred, keepdims=True) / 256.0
    features = centred * lax.rsqrt(variance + 1e-05)
    feature_row = jnp.concatenate([features[0:1], features[1:2]], axis=1)
    feature_rows = jnp.broadcast_to(feature_row, (16, 256))
    noise_high, noise_low = split(noise_w[...])
    shift = dot_split(stacked(feature_rows), noise_high, noise_low)[0:1]
    cond_both = stacked(layer_norm(cond[...] + shift))

    loads[4].wait()

    def ada_step(step, _):
        columns = pl.ds(pl.multiple_of(step * 256, 256), 256)
        high, low = split(ada_w[:, columns])
        ada[:, columns] = dot_split(cond_both, high, low)
        return 0

    lax.fori_loop(0, 2 * D // 256, ada_step, 0)
    loads[5].wait()
    modulated[...] = (
        sigmoid(ada[:, :D]) * layer_norm(tokens[...]) + ada[:, D:]
    ).reshape(SLICES, SLICE_ROWS, D)

    pl.semaphore_wait(barrier, expected)

    def block_copy(step, piece):
        target_row = 2 * lax.rem(row // 2 + step, 8) + lax.rem(col_y, 2)
        return pltpu.make_async_remote_copy(
            src_ref=modulated.at[piece],
            dst_ref=block.at[piece],
            send_sem=block_send.at[step],
            recv_sem=block_recv.at[piece],
            device_id=(target_row, row, seed),
            device_id_type=MESH,
        )

    @pl.when(is_source)
    def _():
        def send(step, _):
            place = 7 - step

            @pl.when(jnp.logical_not((place == 0) & to_self))
            def _():
                block_copy(place, col_y).start()

            return 0

        lax.fori_loop(0, 8, send, 0)

    @pl.when(is_source & to_self)
    def _():
        block[pl.ds(col_y, 1)] = modulated[pl.ds(col_y, 1)]

    mod_both = stacked(modulated[...].reshape(TOK, D))
    loads[6].wait()

    def query_step(step, _):
        columns = pl.ds(pl.multiple_of(step * 256, 256), 256)
        high, low = split(qg_w[:, columns])
        result = dot_split(mod_both, high, low) * (HEAD_DIM**-0.5)
        q_t[columns, :] = result.T
        return 0

    lax.fori_loop(0, D // 256, query_step, 0)

    def gate_step(step, _):
        columns = pl.ds(pl.multiple_of(step * 256, 256), 256)
        high, low = split(qg_w[:, pl.ds(pl.multiple_of(D + step * 256, 256), 256)])
        gates[:, columns] = sigmoid(dot_split(mod_both, high, low))
        return 0

    lax.fori_loop(0, D // 256, gate_step, 0)
    window_row = lax.broadcasted_iota(jnp.int32, (256, TOK), 0)

    def window_of(head):
        return jnp.minimum(head * HEAD_DIM // 128, D // 128 - 2)

    def query_mask(head, _):
        start = pl.multiple_of(window_of(head) * 128, 128)
        place = head * HEAD_DIM - start
        inside = (window_row >= place) & (window_row < place + HEAD_DIM)
        high, low = split(jnp.where(inside, q_t[pl.ds(start, 256), :], 0.0))
        q_high[head] = high
        q_low[head] = low
        return 0

    lax.fori_loop(0, HEADS, query_mask, 0)

    for number in (7, 8, 9, 10):
        loads[number].wait()
    chain_f = chain[...].astype(F32)
    residue_f = residue[...].astype(F32)
    place = lax.broadcasted_iota(jnp.int32, (N_ROW, TOK), 0)

    def pick(values, which):
        chosen = jnp.sum(jnp.where(place == which, values, 0.0), axis=0, keepdims=True)
        return jnp.broadcast_to(chosen, (TOK, TOK))

    same = pick(chain_f, row) == pick(chain_f, col).T
    offset = jnp.clip(pick(residue_f, row) - pick(residue_f, col).T, -REL, REL) + REL
    bucket = jnp.where(same, offset, 2.0 * REL + 1.0).astype(jnp.int32)
    wide = jnp.concatenate(
        [table[...], jnp.zeros((HEADS, 128 - 2 * REL - 2), F32)], axis=1
    )
    table_rows = [wide[head : head + 1] for head in range(HEADS)]
    for head in range(HEADS):
        rel = jnp.take_along_axis(
            jnp.broadcast_to(table_rows[head], (TOK, 128)), bucket, axis=1
        )
        scores_bias[head] = bias[head].astype(F32).T + rel

    loads[11].wait()

    def out_gate_step(step, _):
        columns = pl.ds(pl.multiple_of(step * 256, 256), 256)
        high, low = split(og_w[:, columns])
        out_gate[:, columns] = sigmoid(dot_split(cond_both, high, low))
        return 0

    lax.fori_loop(0, D // 256, out_gate_step, 0)
    loads[12].wait()

    def kv_split(step, _):
        columns = pl.ds(pl.multiple_of(step * 256, 256), 256)
        high, low = split(kv_w[:, columns])
        kv_high[:, columns] = high
        kv_low[:, columns] = low
        return 0

    lax.fori_loop(0, 2 * D // 256, kv_split, 0)

    def mate_copy(piece):
        return pltpu.make_async_remote_copy(
            src_ref=block.at[piece],
            dst_ref=block.at[piece],
            send_sem=mate_send.at[piece],
            recv_sem=mate_recv.at[piece],
            device_id=mate,
            device_id_type=MESH,
        )

    def pass_on(step, _):
        piece = 2 * step + core

        @pl.when(jnp.logical_not(to_self & (piece == col_y)))
        def _():
            block_copy(0, piece).wait_recv()

        mate_copy(piece).start()
        return 0

    lax.fori_loop(0, SLICES // 2, pass_on, 0)

    def from_mate(step, _):
        mate_copy(2 * step + 1 - core).wait_recv()
        return 0

    lax.fori_loop(0, SLICES // 2, from_mate, 0)

    block_both = stacked(block[...].reshape(TOK, D))

    def key_step(step, _):
        columns = pl.ds(pl.multiple_of(step * 256, 256), 256)
        high, low = split(dot_split(block_both, kv_high[:, columns], kv_low[:, columns]))
        k_high[:, columns] = high
        k_low[:, columns] = low
        return 0

    lax.fori_loop(0, D // 256, key_step, 0)

    def value_step(step, _):
        columns = pl.ds(pl.multiple_of(step * 256, 256), 256)
        source = pl.ds(pl.multiple_of(D + step * 256, 256), 256)
        v_t[columns, :] = dot_split(block_both, kv_high[:, source], kv_low[:, source]).T
        return 0

    lax.fori_loop(0, D // 256, value_step, 0)

    ones_rows = jnp.where(lax.broadcasted_iota(jnp.int32, (16, TOK), 0) == 0, 1.0, 0.0)
    tail_row = lax.broadcasted_iota(jnp.int32, (8, TOK), 0)

    def one_head(head):
        keys = pl.ds(pl.multiple_of(window_of(head) * 128, 128), 256)
        keys_high, keys_low = k_high[:, keys], k_low[:, keys]
        queries = q_high[head]
        scores = (
            mul(keys_high, queries)
            + mul(keys_low, queries)
            + mul(keys_high, q_low[head])
            + scores_bias[head]
        )
        top = jnp.max(scores, axis=0, keepdims=True)
        weights_high, weights_low = split(jnp.exp(scores - top))
        values = v_t[pl.ds(pl.multiple_of(head * HEAD_DIM, 16), HEAD_DIM), :]
        values_high, values_low = split(jnp.concatenate([values, ones_rows], axis=0))
        sums = (
            mul(values_high, weights_high)
            + mul(values_low, weights_high)
            + mul(values_high, weights_low)
        )
        tail = jnp.where(tail_row == 1, top, sums[HEAD_DIM:MSG_ROWS])
        return sums[:HEAD_DIM], tail

    def part_copy(head):
        return pltpu.make_async_remote_copy(
            src_ref=parts_out.at[head],
            dst_ref=parts_in.at[col],
            send_sem=part_send.at[head],
            recv_sem=part_recv.at[col],
            device_id=(row, head, seed),
            device_id_type=MESH,
        )

    def head_group(group, _):
        for member in range(3):
            head = lax.rem(col + 1 + group * 3 + member, HEADS)
            sums, tail = one_head(head)
            parts_out[head, :HEAD_DIM] = sums
            parts_out[head, HEAD_DIM:] = tail
            part_copy(head).start()
        return 0

    lax.fori_loop(0, 5, head_group, 0)
    sums, tail = one_head(col)
    parts_in[col, :HEAD_DIM] = sums
    parts_in[col, HEAD_DIM:] = tail

    def part_arrived(step, _):
        other = lax.rem(col + N_COL - step, N_COL)
        pltpu.make_async_remote_copy(
            src_ref=parts_out.at[other],
            dst_ref=parts_in.at[other],
            send_sem=part_send.at[other],
            recv_sem=part_recv.at[other],
            device_id=(row, other, seed),
            device_id_type=MESH,
        ).wait_recv()
        return 0

    lax.fori_loop(1, N_COL, part_arrived, 0)
    tops = parts_in[:, HEAD_DIM + 1 : HEAD_DIM + 2, :]
    factors = jnp.exp(tops - jnp.max(tops, axis=0, keepdims=True))
    total = jnp.sum(factors * parts_in[:, HEAD_DIM : HEAD_DIM + 1, :], axis=0)
    weighted = jnp.sum(factors * parts_in[:, :HEAD_DIM, :], axis=0)
    attended[pl.ds(col, 1)] = (weighted / total)[None]

    def att_copy(other, place):
        return pltpu.make_async_remote_copy(
            src_ref=attended.at[place],
            dst_ref=attended.at[place],
            send_sem=att_send.at[other],
            recv_sem=att_recv.at[place],
            device_id=(row, other, seed),
            device_id_type=MESH,
        )

    def att_start(step, _):
        att_copy(lax.rem(col + step, N_COL), col).start()
        return 0

    lax.fori_loop(1, N_COL, att_start, 0)
    loads[13].wait()

    def att_arrived(step, _):
        other = lax.rem(col + N_COL - step, N_COL)
        att_copy(other, other).wait_recv()
        return 0

    lax.fori_loop(1, N_COL, att_arrived, 0)
    gated_both = stacked(gates[...] * attended[...].reshape(D, TOK).T)

    def out_step(step, _):
        columns = pl.ds(pl.multiple_of(step * 256, 256), 256)
        high, low = split(out_w[:, columns])
        out_ref[:, columns] = tokens[:, columns] + out_gate[:, columns] * dot_split(
            gated_both, high, low
        )
        return 0

    lax.fori_loop(0, D // 256, out_step, 0)

    @pl.when(is_source)
    def _():
        def sent(step, _):
            @pl.when(jnp.logical_not((step == 0) & to_self))
            def _():
                block_copy(step, col_y).wait_send()

            return 0

        lax.fori_loop(0, 8, sent, 0)

    def mate_sent(step, _):
        mate_copy(2 * step + core).wait_send()
        return 0

    lax.fori_loop(0, SLICES // 2, mate_sent, 0)

    def parts_sent(step, _):
        other = lax.rem(col + step, N_COL)
        part_copy(other).wait_send()
        att_copy(other, col).wait_send()
        return 0

    lax.fori_loop(1, N_COL, parts_sent, 0)


def body(
    tokens_act,
    single_cond,
    noise_level,
    fourier_freq,
    fourier_phase,
    noise_weight,
    ada_weight,
    query_gate_weight,
    kv_weight,
    out_weight,
    out_gate_weight,
    pair_bias,
    relpos_table,
    chain_id,
    residue_index,
):
    hbm = pl.BlockSpec(memory_space=pl.ANY)
    vmem = pltpu.VMEM
    dma = pltpu.SemaphoreType.DMA
    return pl.pallas_call(
        kernel,
        name="attention_block",
        out_shape=jax.ShapeDtypeStruct((TOK, D), F32),
        in_specs=[hbm, hbm, pl.BlockSpec(memory_space=pltpu.SMEM)] + [hbm] * 12,
        out_specs=pl.BlockSpec(memory_space=pltpu.VMEM),
        scratch_shapes=[
            vmem((TOK, D), F32),
            vmem((TOK, C_S), F32),
            vmem((2, 128), F32),
            vmem((2, 128), F32),
            vmem((256, C_S), F32),
            vmem((C_S, 2 * D), F32),
            vmem((D, 2 * D), F32),
            vmem((D, 2 * D), F32),
            vmem((D, D), F32),
            vmem((C_S, D), F32),
            vmem((HEADS, TOK, TOK), BF16),
            vmem((HEADS, 2 * REL + 2), F32),
            vmem((N_ROW, TOK), jnp.int32),
            vmem((N_ROW, TOK), jnp.int32),
            vmem((TOK, 2 * D), F32),
            vmem((SLICES, SLICE_ROWS, D), F32),
            vmem((SLICES, SLICE_ROWS, D), F32),
            vmem((HEADS, 256, TOK), BF16),
            vmem((HEADS, 256, TOK), BF16),
            vmem((TOK, D), F32),
            vmem((TOK, D), F32),
            vmem((D, TOK), F32),
            vmem((D, TOK), F32),
            vmem((TOK, D), BF16),
            vmem((TOK, D), BF16),
            vmem((D, 2 * D), BF16),
            vmem((D, 2 * D), BF16),
            vmem((HEADS, TOK, TOK), F32),
            vmem((HEADS, MSG_ROWS, TOK), F32),
            vmem((N_COL, MSG_ROWS, TOK), F32),
            vmem((HEADS, HEAD_DIM, TOK), F32),
            dma((14,)),
            dma((8,)),
            dma((SLICES,)),
            dma((SLICES,)),
            dma((SLICES,)),
            dma((N_COL,)),
            dma((N_COL,)),
            dma((N_COL,)),
            dma((N_COL,)),
        ],
        compiler_params=pltpu.CompilerParams(
            collective_id=0, has_side_effects=True, vmem_limit_bytes=48 * 1024 * 1024
        ),
    )(
        tokens_act,
        single_cond,
        noise_level.reshape(1, 1),
        fourier_freq.reshape(2, 128),
        fourier_phase.reshape(2, 128),
        noise_weight,
        ada_weight,
        query_gate_weight,
        kv_weight,
        out_weight,
        out_gate_weight,
        pair_bias,
        relpos_table,
        chain_id.reshape(N_ROW, TOK),
        residue_index.reshape(N_ROW, TOK),
    )


def solution(mesh):
    in_specs = (
        P(("seed", "row"), None),
        P(("seed", "row"), None),
        P("seed"),
        P(),
        P(),
        P(),
        P(),
        P(),
        P(),
        P(),
        P(),
        P(None, "row", "col"),
        P(),
        P(),
        P(),
    )
    out_specs = P(("seed", "row"), None)
    return jax.shard_map(body, mesh=mesh, in_specs=in_specs, out_specs=out_specs, check_vma=False)
```

```python
import jax
import jax.numpy as jnp
from jax import lax
from jax.experimental import pallas as pl
from jax.experimental.pallas import tpu as pltpu
from jax.sharding import PartitionSpec as P

D = 768
HEADS = 16
HEAD_DIM = 48
C_S = 384
REL = 32
TOK = 128
N_ROW = 16
N_COL = 16
Z = 8
PIECES = 2
PIECE_ROWS = TOK // 2 // PIECES
MSG_ROWS = 56
MESH = pl.DeviceIdType.MESH
F32 = jnp.float32
BF16 = jnp.bfloat16


def split(value):
    high = value.astype(BF16)
    low = (value - high.astype(F32)).astype(BF16)
    return high, low


def mul(left, right):
    return jnp.dot(left, right, preferred_element_type=F32)


def stacked(value):
    high, low = split(value)
    return jnp.concatenate([high, low], axis=0)


def dot_split(both, right_high, right_low):
    rows = both.shape[0] // 2
    first = mul(both, right_high)
    return first[:rows] + first[rows:] + mul(both[:rows], right_low)


def layer_norm(inputs):
    average = jnp.mean(inputs, axis=-1, keepdims=True)
    centred = inputs - average
    variance = jnp.mean(centred * centred, axis=-1, keepdims=True)
    return centred * lax.rsqrt(variance + 1e-05)


def sigmoid(value):
    return 1.0 / (1.0 + jnp.exp(-value))


def kernel(
    tokens_hbm,
    cond_hbm,
    noise_ref,
    freq_hbm,
    phase_hbm,
    noise_w_hbm,
    ada_w_hbm,
    qg_w_hbm,
    kv_w_hbm,
    out_w_hbm,
    og_w_hbm,
    bias_hbm,
    table_hbm,
    chain_hbm,
    residue_hbm,
    out_ref,
    tokens,
    cond,
    freq,
    phase,
    noise_w,
    ada_w,
    qg_w,
    kv_w,
    out_w,
    og_w,
    bias,
    table,
    chain,
    residue,
    ada,
    modulated,
    block,
    q_high,
    q_low,
    gates,
    out_gate,
    q_t,
    v_t,
    k_high,
    k_low,
    kv_high,
    kv_low,
    scores_bias,
    parts_out,
    parts_in,
    attended,
    load_sems,
    source_send,
    onward_send,
    mate_send,
    block_recv,
    part_send,
    part_recv,
    att_send,
    att_recv,
):
    row = lax.axis_index("row")
    col = lax.axis_index("col")
    seed = lax.axis_index("seed")
    z, core = row // 2, lax.rem(row, 2)
    mate = (row + 1 - 2 * core, col, seed)
    is_source = row == col
    far = lax.rem(z + Z - col // 2, Z)
    is_relay = (far == 2) | (far == 6)
    onward = jnp.where(far == 2, 1, -1)
    is_long = is_relay & ((far == 2) == (core == 0))

    def along(delta, which):
        return (2 * lax.rem(z + Z + delta, Z) + which, col, seed)

    pairs = (
        (cond_hbm, cond),
        (freq_hbm, freq),
        (phase_hbm, phase),
        (noise_w_hbm, noise_w),
        (ada_w_hbm, ada_w),
        (tokens_hbm, tokens),
        (qg_w_hbm, qg_w),
        (chain_hbm, chain),
        (residue_hbm, residue),
        (table_hbm, table),
        (bias_hbm, bias),
        (og_w_hbm, og_w),
        (kv_w_hbm, kv_w),
        (out_w_hbm, out_w),
    )
    loads = {}
    for number, (source, target) in enumerate(pairs):
        copy = pltpu.make_async_copy(source, target, load_sems.at[number])
        copy.start()
        loads[number] = copy

    barrier = pltpu.get_barrier_semaphore()

    def greet(step, _):
        pl.semaphore_signal(
            barrier,
            inc=1,
            device_id=(row, lax.rem(col + step, N_COL), seed),
            device_id_type=MESH,
        )
        return 0

    sender_delta = jnp.where(
        far == 3, -1, jnp.where(far == 5, 1, jnp.where(core == 0, -2, 2))
    )
    is_onward = (far >= 3) & (far <= 5)
    sender = jnp.where(is_onward, along(sender_delta, core)[0], col)

    @pl.when(far != 0)
    def _():
        pl.semaphore_signal(
            barrier, inc=1, device_id=(sender, col, seed), device_id_type=MESH
        )

    pl.semaphore_signal(barrier, inc=1, device_id=mate, device_id_type=MESH)
    lax.fori_loop(1, N_COL, greet, 0)
    expected = (
        N_COL
        + jnp.where(is_source, 8, 0)
        + jnp.where(is_relay, 1, 0)
        + jnp.where(is_long, 1, 0)
    )

    for number in (0, 1, 2, 3):
        loads[number].wait()
    level = jnp.full((2, 128), noise_ref[0, 0], F32)
    noise_scaled = 0.25 * jnp.log(level / 16.0)
    features = jnp.cos(2.0 * jnp.pi * (noise_scaled * freq[...] + phase[...]))
    average = jnp.sum(features, keepdims=True) / 256.0
    centred = features - average
    variance = jnp.sum(centred * centred, keepdims=True) / 256.0
    features = centred * lax.rsqrt(variance + 1e-05)
    feature_row = jnp.concatenate([features[0:1], features[1:2]], axis=1)
    feature_rows = jnp.broadcast_to(feature_row, (16, 256))
    noise_high, noise_low = split(noise_w[...])
    shift = dot_split(stacked(feature_rows), noise_high, noise_low)[0:1]
    cond_both = stacked(layer_norm(cond[...] + shift))

    loads[4].wait()

    def ada_step(step, _):
        columns = pl.ds(pl.multiple_of(step * 256, 256), 256)
        high, low = split(ada_w[:, columns])
        ada[:, columns] = dot_split(cond_both, high, low)
        return 0

    lax.fori_loop(0, 2 * D // 256, ada_step, 0)
    loads[5].wait()
    modulated[...] = (
        sigmoid(ada[:, :D]) * layer_norm(tokens[...]) + ada[:, D:]
    ).reshape(2, PIECES, PIECE_ROWS, D)

    pl.semaphore_wait(barrier, expected)

    def source_copy(place, half, piece):
        return pltpu.make_async_remote_copy(
            src_ref=modulated.at[half, piece],
            dst_ref=block.at[half, piece],
            send_sem=source_send.at[place, half, piece],
            recv_sem=block_recv.at[half, piece],
            device_id=along((2, -2, 1, -1)[place], half),
            device_id_type=MESH,
        )

    def onward_copy(place, piece):
        return pltpu.make_async_remote_copy(
            src_ref=block.at[core, piece],
            dst_ref=block.at[core, piece],
            send_sem=onward_send.at[place, piece],
            recv_sem=block_recv.at[core, piece],
            device_id=along(onward * (place + 1), core),
            device_id_type=MESH,
        )

    def mate_copy(source, half, piece):
        return pltpu.make_async_remote_copy(
            src_ref=source.at[half, piece],
            dst_ref=block.at[half, piece],
            send_sem=mate_send.at[half, piece],
            recv_sem=block_recv.at[half, piece],
            device_id=mate,
            device_id_type=MESH,
        )

    def arrived(half, piece):
        mate_copy(block, half, piece).wait_recv()

    @pl.when(is_source)
    def _():
        for places in ((0, 1), (2, 3)):
            for piece in range(PIECES):
                for place in places:
                    for half in range(2):
                        source_copy(place, half, piece).start()
            if places[0] == 0:
                for piece in range(PIECES):
                    for half in range(2):
                        mate_copy(modulated, half, piece).start()
        block[...] = modulated[...]

    @pl.when(is_relay)
    def _():
        for piece in range(PIECES):
            arrived(core, piece)
            onward_copy(0, piece).start()

            @pl.when(is_long)
            def _():
                onward_copy(1, piece).start()

            mate_copy(block, core, piece).start()

    mod_both = stacked(modulated[...].reshape(TOK, D))
    loads[6].wait()

    def query_step(step, _):
        columns = pl.ds(pl.multiple_of(step * 256, 256), 256)
        high, low = split(qg_w[:, columns])
        result = dot_split(mod_both, high, low) * (HEAD_DIM**-0.5)
        q_t[columns, :] = result.T
        return 0

    lax.fori_loop(0, D // 256, query_step, 0)

    def gate_step(step, _):
        columns = pl.ds(pl.multiple_of(step * 256, 256), 256)
        high, low = split(qg_w[:, pl.ds(pl.multiple_of(D + step * 256, 256), 256)])
        gates[:, columns] = sigmoid(dot_split(mod_both, high, low))
        return 0

    lax.fori_loop(0, D // 256, gate_step, 0)
    window_row = lax.broadcasted_iota(jnp.int32, (256, TOK), 0)

    def window_of(head):
        return jnp.minimum(head * HEAD_DIM // 128, D // 128 - 2)

    def query_mask(head, _):
        start = pl.multiple_of(window_of(head) * 128, 128)
        place = head * HEAD_DIM - start
        inside = (window_row >= place) & (window_row < place + HEAD_DIM)
        high, low = split(jnp.where(inside, q_t[pl.ds(start, 256), :], 0.0))
        q_high[head] = high
        q_low[head] = low
        return 0

    lax.fori_loop(0, HEADS, query_mask, 0)

    for number in (7, 8, 9, 10):
        loads[number].wait()
    chain_f = chain[...].astype(F32)
    residue_f = residue[...].astype(F32)
    place = lax.broadcasted_iota(jnp.int32, (N_ROW, TOK), 0)

    def pick(values, which):
        chosen = jnp.sum(jnp.where(place == which, values, 0.0), axis=0, keepdims=True)
        return jnp.broadcast_to(chosen, (TOK, TOK))

    same = pick(chain_f, row) == pick(chain_f, col).T
    offset = jnp.clip(pick(residue_f, row) - pick(residue_f, col).T, -REL, REL) + REL
    bucket = jnp.where(same, offset, 2.0 * REL + 1.0).astype(jnp.int32)
    wide = jnp.concatenate(
        [table[...], jnp.zeros((HEADS, 128 - 2 * REL - 2), F32)], axis=1
    )
    table_rows = [wide[head : head + 1] for head in range(HEADS)]
    for head in range(HEADS):
        rel = jnp.take_along_axis(
            jnp.broadcast_to(table_rows[head], (TOK, 128)), bucket, axis=1
        )
        scores_bias[head] = bias[head].astype(F32).T + rel

    loads[11].wait()

    def out_gate_step(step, _):
        columns = pl.ds(pl.multiple_of(step * 256, 256), 256)
        high, low = split(og_w[:, columns])
        out_gate[:, columns] = sigmoid(dot_split(cond_both, high, low))
        return 0

    lax.fori_loop(0, D // 256, out_gate_step, 0)
    loads[12].wait()

    def kv_split(step, _):
        columns = pl.ds(pl.multiple_of(step * 256, 256), 256)
        high, low = split(kv_w[:, columns])
        kv_high[:, columns] = high
        kv_low[:, columns] = low
        return 0

    lax.fori_loop(0, 2 * D // 256, kv_split, 0)

    @pl.when((far != 0) & jnp.logical_not(is_relay))
    def _():
        for piece in range(PIECES):
            arrived(core, piece)
            mate_copy(block, core, piece).start()

    @pl.when(far != 0)
    def _():
        for piece in range(PIECES):
            arrived(1 - core, piece)
        for piece in range(PIECES):
            mate_copy(block, core, piece).wait_send()

    @pl.when((far == 0) & jnp.logical_not(is_source))
    def _():
        for piece in range(PIECES):
            for half in range(2):
                arrived(half, piece)

    @pl.when(is_relay)
    def _():
        for piece in range(PIECES):
            onward_copy(0, piece).wait_send()

            @pl.when(is_long)
            def _():
                onward_copy(1, piece).wait_send()

    @pl.when(is_source)
    def _():
        for piece in range(PIECES):
            for half in range(2):
                for place in range(4):
                    source_copy(place, half, piece).wait_send()
                mate_copy(modulated, half, piece).wait_send()

    block_both = stacked(block[...].reshape(TOK, D))

    def key_step(step, _):
        columns = pl.ds(pl.multiple_of(step * 256, 256), 256)
        high, low = split(dot_split(block_both, kv_high[:, columns], kv_low[:, columns]))
        k_high[:, columns] = high
        k_low[:, columns] = low
        return 0

    lax.fori_loop(0, D // 256, key_step, 0)

    def value_step(step, _):
        columns = pl.ds(pl.multiple_of(step * 256, 256), 256)
        source = pl.ds(pl.multiple_of(D + step * 256, 256), 256)
        v_t[columns, :] = dot_split(block_both, kv_high[:, source], kv_low[:, source]).T
        return 0

    lax.fori_loop(0, D // 256, value_step, 0)

    ones_rows = jnp.where(lax.broadcasted_iota(jnp.int32, (16, TOK), 0) == 0, 1.0, 0.0)
    tail_row = lax.broadcasted_iota(jnp.int32, (8, TOK), 0)

    def one_head(head):
        keys = pl.ds(pl.multiple_of(window_of(head) * 128, 128), 256)
        keys_high, keys_low = k_high[:, keys], k_low[:, keys]
        queries = q_high[head]
        scores = (
            mul(keys_high, queries)
            + mul(keys_low, queries)
            + mul(keys_high, q_low[head])
            + scores_bias[head]
        )
        top = jnp.max(scores, axis=0, keepdims=True)
        weights_high, weights_low = split(jnp.exp(scores - top))
        values = v_t[pl.ds(pl.multiple_of(head * HEAD_DIM, 16), HEAD_DIM), :]
        values_high, values_low = split(jnp.concatenate([values, ones_rows], axis=0))
        sums = (
            mul(values_high, weights_high)
            + mul(values_low, weights_high)
            + mul(values_high, weights_low)
        )
        tail = jnp.where(tail_row == 1, top, sums[HEAD_DIM:MSG_ROWS])
        return sums[:HEAD_DIM], tail

    def part_copy(head):
        return pltpu.make_async_remote_copy(
            src_ref=parts_out.at[head],
            dst_ref=parts_in.at[col],
            send_sem=part_send.at[head],
            recv_sem=part_recv.at[col],
            device_id=(row, head, seed),
            device_id_type=MESH,
        )

    def head_group(group, _):
        for member in range(3):
            head = lax.rem(col + 1 + group * 3 + member, HEADS)
            sums, tail = one_head(head)
            parts_out[head, :HEAD_DIM] = sums
            parts_out[head, HEAD_DIM:] = tail
            part_copy(head).start()
        return 0

    lax.fori_loop(0, 5, head_group, 0)
    sums, tail = one_head(col)
    parts_in[col, :HEAD_DIM] = sums
    parts_in[col, HEAD_DIM:] = tail

    def part_arrived(step, _):
        other = lax.rem(col + N_COL - step, N_COL)
        pltpu.make_async_remote_copy(
            src_ref=parts_out.at[other],
            dst_ref=parts_in.at[other],
            send_sem=part_send.at[other],
            recv_sem=part_recv.at[other],
            device_id=(row, other, seed),
            device_id_type=MESH,
        ).wait_recv()
        return 0

    lax.fori_loop(1, N_COL, part_arrived, 0)
    def part_sent(step, _):
        part_copy(lax.rem(col + step, N_COL)).wait_send()
        return 0

    lax.fori_loop(1, N_COL, part_sent, 0)
    tops = parts_in[:, HEAD_DIM + 1 : HEAD_DIM + 2, :]
    factors = jnp.exp(tops - jnp.max(tops, axis=0, keepdims=True))
    total = jnp.sum(factors * parts_in[:, HEAD_DIM : HEAD_DIM + 1, :], axis=0)
    weighted = jnp.sum(factors * parts_in[:, :HEAD_DIM, :], axis=0)
    attended[pl.ds(col, 1)] = (weighted / total)[None]

    def att_copy(other, place):
        return pltpu.make_async_remote_copy(
            src_ref=attended.at[place],
            dst_ref=attended.at[place],
            send_sem=att_send.at[other],
            recv_sem=att_recv.at[place],
            device_id=(row, other, seed),
            device_id_type=MESH,
        )

    def att_start(step, _):
        att_copy(lax.rem(col + step, N_COL), col).start()
        return 0

    lax.fori_loop(1, N_COL, att_start, 0)
    loads[13].wait()

    def att_arrived(step, _):
        other = lax.rem(col + N_COL - step, N_COL)
        att_copy(other, other).wait_recv()
        return 0

    lax.fori_loop(1, N_COL, att_arrived, 0)
    gated_both = stacked(gates[...] * attended[...].reshape(D, TOK).T)

    def out_step(step, _):
        columns = pl.ds(pl.multiple_of(step * 256, 256), 256)
        high, low = split(out_w[:, columns])
        out_ref[:, columns] = tokens[:, columns] + out_gate[:, columns] * dot_split(
            gated_both, high, low
        )
        return 0

    lax.fori_loop(0, D // 256, out_step, 0)

    def att_sent(step, _):
        att_copy(lax.rem(col + step, N_COL), col).wait_send()
        return 0

    lax.fori_loop(1, N_COL, att_sent, 0)


def body(
    tokens_act,
    single_cond,
    noise_level,
    fourier_freq,
    fourier_phase,
    noise_weight,
    ada_weight,
    query_gate_weight,
    kv_weight,
    out_weight,
    out_gate_weight,
    pair_bias,
    relpos_table,
    chain_id,
    residue_index,
):
    hbm = pl.BlockSpec(memory_space=pltpu.HBM)
    vmem = pltpu.VMEM
    dma = pltpu.SemaphoreType.DMA
    return pl.pallas_call(
        kernel,
        name="attention_block",
        out_shape=jax.ShapeDtypeStruct((TOK, D), F32),
        in_specs=[hbm, hbm, pl.BlockSpec(memory_space=pltpu.SMEM)] + [hbm] * 12,
        out_specs=pl.BlockSpec(memory_space=pltpu.VMEM),
        scratch_shapes=[
            vmem((TOK, D), F32),
            vmem((TOK, C_S), F32),
            vmem((2, 128), F32),
            vmem((2, 128), F32),
            vmem((256, C_S), F32),
            vmem((C_S, 2 * D), F32),
            vmem((D, 2 * D), F32),
            vmem((D, 2 * D), F32),
            vmem((D, D), F32),
            vmem((C_S, D), F32),
            vmem((HEADS, TOK, TOK), BF16),
            vmem((HEADS, 2 * REL + 2), F32),
            vmem((N_ROW, TOK), jnp.int32),
            vmem((N_ROW, TOK), jnp.int32),
            vmem((TOK, 2 * D), F32),
            vmem((2, PIECES, PIECE_ROWS, D), F32),
            vmem((2, PIECES, PIECE_ROWS, D), F32),
            vmem((HEADS, 256, TOK), BF16),
            vmem((HEADS, 256, TOK), BF16),
            vmem((TOK, D), F32),
            vmem((TOK, D), F32),
            vmem((D, TOK), F32),
            vmem((D, TOK), F32),
            vmem((TOK, D), BF16),
            vmem((TOK, D), BF16),
            vmem((D, 2 * D), BF16),
            vmem((D, 2 * D), BF16),
            vmem((HEADS, TOK, TOK), F32),
            vmem((HEADS, MSG_ROWS, TOK), F32),
            vmem((N_COL, MSG_ROWS, TOK), F32),
            vmem((HEADS, HEAD_DIM, TOK), F32),
            dma((14,)),
            dma((4, 2, PIECES)),
            dma((2, PIECES)),
            dma((2, PIECES)),
            dma((2, PIECES)),
            dma((N_COL,)),
            dma((N_COL,)),
            dma((N_COL,)),
            dma((N_COL,)),
        ],
        compiler_params=pltpu.CompilerParams(
            collective_id=0, has_side_effects=True, vmem_limit_bytes=60 * 1024 * 1024
        ),
    )(
        tokens_act,
        single_cond,
        noise_level.reshape(1, 1),
        fourier_freq.reshape(2, 128),
        fourier_phase.reshape(2, 128),
        noise_weight,
        ada_weight,
        query_gate_weight,
        kv_weight,
        out_weight,
        out_gate_weight,
        pair_bias,
        relpos_table,
        chain_id.reshape(N_ROW, TOK),
        residue_index.reshape(N_ROW, TOK),
    )


def solution(mesh):
    in_specs = (
        P(("seed", "row"), None),
        P(("seed", "row"), None),
        P("seed"),
        P(),
        P(),
        P(),
        P(),
        P(),
        P(),
        P(),
        P(),
        P(None, "row", "col"),
        P(),
        P(),
        P(),
    )
    out_specs = P(("seed", "row"), None)
    return jax.shard_map(body, mesh=mesh, in_specs=in_specs, out_specs=out_specs, check_vma=False)
```

```python
import jax
import jax.numpy as jnp
from jax import lax
from jax.experimental import pallas as pl
from jax.experimental.pallas import tpu as pltpu
from jax.sharding import PartitionSpec as P

D = 768
HEADS = 16
HEAD_DIM = 48
C_S = 384
REL = 32
TOK = 128
N_ROW = 16
N_COL = 16
Z = 8
Y = 8
YS = (4, 3, 5, 2, 6, 1, 7)
PIECES = 4
PIECE_ROWS = TOK // 2 // PIECES
MSG_ROWS = 56
MESH = pl.DeviceIdType.MESH
F32 = jnp.float32
BF16 = jnp.bfloat16


def split(value):
    high = value.astype(BF16)
    low = (value - high.astype(F32)).astype(BF16)
    return high, low


def mul(left, right):
    return jnp.dot(left, right, preferred_element_type=F32)


def stacked(value):
    high, low = split(value)
    return jnp.concatenate([high, low], axis=0)


def dot_split(both, right_high, right_low):
    rows = both.shape[0] // 2
    first = mul(both, right_high)
    return first[:rows] + first[rows:] + mul(both[:rows], right_low)


def layer_norm(inputs):
    average = jnp.mean(inputs, axis=-1, keepdims=True)
    centred = inputs - average
    variance = jnp.mean(centred * centred, axis=-1, keepdims=True)
    return centred * lax.rsqrt(variance + 1e-05)


def sigmoid(value):
    return 1.0 / (1.0 + jnp.exp(-value))


def kernel(
    tokens_hbm,
    cond_hbm,
    noise_ref,
    freq_hbm,
    phase_hbm,
    noise_w_hbm,
    ada_w_hbm,
    qg_w_hbm,
    kv_w_hbm,
    out_w_hbm,
    og_w_hbm,
    bias_hbm,
    table_hbm,
    chain_hbm,
    residue_hbm,
    out_ref,
    tokens,
    cond,
    freq,
    phase,
    noise_w,
    ada_w,
    qg_w,
    kv_w,
    out_w,
    og_w,
    bias,
    table,
    chain,
    residue,
    ada,
    modulated,
    block,
    q_high,
    q_low,
    gates,
    out_gate,
    q_t,
    v_t,
    k_high,
    k_low,
    kv_high,
    kv_low,
    scores_bias,
    parts_out,
    parts_in,
    parts_pair,
    attended,
    load_sems,
    source_send,
    onward_send,
    mate_send,
    block_recv,
    pair_send,
    pair_recv,
    part_send,
    part_recv,
    att_send,
    across_send,
    att_recv,
):
    row = lax.axis_index("row")
    col = lax.axis_index("col")
    seed = lax.axis_index("seed")
    z, core = row // 2, lax.rem(row, 2)
    mate = (row + 1 - 2 * core, col, seed)
    col_y, col_x = col // 2, lax.rem(col, 2)
    partner = (row, 2 * col_y + 1 - col_x, seed)
    is_source = row == col
    far = lax.rem(z + Z - col // 2, Z)
    is_relay = (far == 2) | (far == 6)
    onward = jnp.where(far == 2, 1, -1)
    is_long = is_relay & ((far == 2) == (core == 0))

    def along(delta, which):
        return (2 * lax.rem(z + Z + delta, Z) + which, col, seed)

    pairs = (
        (freq_hbm, freq),
        (phase_hbm, phase),
        (noise_w_hbm, noise_w),
        (cond_hbm, cond),
        (tokens_hbm, tokens),
        (ada_w_hbm, ada_w),
        (qg_w_hbm, qg_w),
        (chain_hbm, chain),
        (residue_hbm, residue),
        (table_hbm, table),
        (bias_hbm, bias),
        (og_w_hbm, og_w),
        (kv_w_hbm, kv_w),
        (out_w_hbm, out_w),
    )
    loads = {
        number: pltpu.make_async_copy(source, target, load_sems.at[number])
        for number, (source, target) in enumerate(pairs)
    }
    for number in range(6):
        loads[number].start()

    barrier = pltpu.get_barrier_semaphore()

    def greet(step, _):
        pl.semaphore_signal(
            barrier,
            inc=1,
            device_id=(row, lax.rem(col + 2 * step, N_COL), seed),
            device_id_type=MESH,
        )
        return 0

    sender_delta = jnp.where(
        far == 3, -1, jnp.where(far == 5, 1, jnp.where(core == 0, -2, 2))
    )
    is_onward = (far >= 3) & (far <= 5)
    sender = jnp.where(is_onward, along(sender_delta, core)[0], col)

    @pl.when(far != 0)
    def _():
        pl.semaphore_signal(
            barrier, inc=1, device_id=(sender, col, seed), device_id_type=MESH
        )

    pl.semaphore_signal(barrier, inc=1, device_id=mate, device_id_type=MESH)
    pl.semaphore_signal(barrier, inc=1, device_id=partner, device_id_type=MESH)
    lax.fori_loop(1, Y, greet, 0)
    expected = (
        Y
        + 1
        + jnp.where(is_source, 8, 0)
        + jnp.where(is_relay, 1, 0)
        + jnp.where(is_long, 1, 0)
    )

    for number in (0, 1):
        loads[number].wait()
    level = jnp.full((2, 128), noise_ref[0, 0], F32)
    noise_scaled = 0.25 * jnp.log(level / 16.0)
    features = jnp.cos(2.0 * jnp.pi * (noise_scaled * freq[...] + phase[...]))
    feature_row = layer_norm(jnp.concatenate([features[0:1], features[1:2]], axis=1))
    feature_rows = jnp.broadcast_to(feature_row, (16, 256))
    loads[2].wait()
    noise_high, noise_low = split(noise_w[...])
    shift = dot_split(stacked(feature_rows), noise_high, noise_low)[0:1]
    loads[3].wait()
    cond_both = stacked(layer_norm(cond[...] + shift))
    loads[4].wait()
    tokens_norm = layer_norm(tokens[...])
    loads[5].wait()
    for number in range(6, len(pairs)):
        loads[number].start()

    def ada_step(step, _):
        columns = pl.ds(pl.multiple_of(step * 256, 256), 256)
        high, low = split(ada_w[:, columns])
        ada[:, columns] = dot_split(cond_both, high, low)
        return 0

    lax.fori_loop(0, 2 * D // 256, ada_step, 0, unroll=True)
    modulated[...] = (sigmoid(ada[:, :D]) * tokens_norm + ada[:, D:]).reshape(2, PIECES, PIECE_ROWS, D)

    pl.semaphore_wait(barrier, expected)

    def source_copy(place, half, piece):
        return pltpu.make_async_remote_copy(
            src_ref=modulated.at[half, piece],
            dst_ref=block.at[half, piece],
            send_sem=source_send.at[place, half, piece],
            recv_sem=block_recv.at[half, piece],
            device_id=along((2, -2, 1, -1)[place], half),
            device_id_type=MESH,
        )

    def onward_copy(place, piece):
        return pltpu.make_async_remote_copy(
            src_ref=block.at[core, piece],
            dst_ref=block.at[core, piece],
            send_sem=onward_send.at[place, piece],
            recv_sem=block_recv.at[core, piece],
            device_id=along(onward * (place + 1), core),
            device_id_type=MESH,
        )

    def mate_copy(source, half, piece):
        return pltpu.make_async_remote_copy(
            src_ref=source.at[half, piece],
            dst_ref=block.at[half, piece],
            send_sem=mate_send.at[half, piece],
            recv_sem=block_recv.at[half, piece],
            device_id=mate,
            device_id_type=MESH,
        )

    def arrived(half, piece):
        mate_copy(block, half, piece).wait_recv()

    @pl.when(is_source)
    def _():
        for places in ((0, 1), (2, 3)):
            for piece in range(PIECES):
                for place in places:
                    for half in range(2):
                        source_copy(place, half, piece).start()
            if places[0] == 0:
                for piece in range(PIECES):
                    for half in range(2):
                        mate_copy(modulated, half, piece).start()
        block[...] = modulated[...]

    @pl.when(is_relay)
    def _():
        for piece in range(PIECES):
            arrived(core, piece)

            @pl.when(is_long)
            def _():
                onward_copy(1, piece).start()

            onward_copy(0, piece).start()
            mate_copy(block, core, piece).start()

    mod_both = stacked(modulated[...].reshape(TOK, D))
    loads[6].wait()

    def query_step(step, _):
        columns = pl.ds(pl.multiple_of(step * 256, 256), 256)
        high, low = split(qg_w[:, columns])
        result = dot_split(mod_both, high, low) * (HEAD_DIM**-0.5)
        q_t[columns, :] = result.T
        return 0

    lax.fori_loop(0, D // 256, query_step, 0, unroll=True)

    def gate_step(step, _):
        columns = pl.ds(pl.multiple_of(step * 256, 256), 256)
        high, low = split(qg_w[:, pl.ds(pl.multiple_of(D + step * 256, 256), 256)])
        gates[:, columns] = sigmoid(dot_split(mod_both, high, low))
        return 0

    lax.fori_loop(0, D // 256, gate_step, 0, unroll=True)
    window_row = lax.broadcasted_iota(jnp.int32, (256, TOK), 0)

    def window_of(head):
        return jnp.minimum(head * HEAD_DIM // 128, D // 128 - 2)

    def query_mask(head, _):
        start = pl.multiple_of(window_of(head) * 128, 128)
        place = head * HEAD_DIM - start
        inside = (window_row >= place) & (window_row < place + HEAD_DIM)
        high, low = split(jnp.where(inside, q_t[pl.ds(start, 256), :], 0.0))
        q_high[head] = high
        q_low[head] = low
        return 0

    lax.fori_loop(0, HEADS, query_mask, 0)

    for number in (7, 8, 9, 10):
        loads[number].wait()
    chain_f = chain[...].astype(F32)
    residue_f = residue[...].astype(F32)
    place = lax.broadcasted_iota(jnp.int32, (N_ROW, TOK), 0)

    def pick(values, which):
        chosen = jnp.sum(jnp.where(place == which, values, 0.0), axis=0, keepdims=True)
        return jnp.broadcast_to(chosen, (TOK, TOK))

    same = pick(chain_f, row) == pick(chain_f, col).T
    offset = jnp.clip(pick(residue_f, row) - pick(residue_f, col).T, -REL, REL) + REL
    bucket = jnp.where(same, offset, 2.0 * REL + 1.0).astype(jnp.int32)
    wide = jnp.concatenate(
        [table[...], jnp.zeros((HEADS, 128 - 2 * REL - 2), F32)], axis=1
    )
    table_rows = [wide[head : head + 1] for head in range(HEADS)]
    for head in range(HEADS):
        rel = jnp.take_along_axis(
            jnp.broadcast_to(table_rows[head], (TOK, 128)), bucket, axis=1
        )
        scores_bias[head] = bias[head].astype(F32).T + rel

    loads[11].wait()

    def out_gate_step(step, _):
        columns = pl.ds(pl.multiple_of(step * 256, 256), 256)
        high, low = split(og_w[:, columns])
        out_gate[:, columns] = sigmoid(dot_split(cond_both, high, low))
        return 0

    lax.fori_loop(0, D // 256, out_gate_step, 0, unroll=True)
    loads[12].wait()

    def kv_split(step, _):
        columns = pl.ds(pl.multiple_of(step * 256, 256), 256)
        high, low = split(kv_w[:, columns])
        kv_high[:, columns] = high
        kv_low[:, columns] = low
        return 0

    lax.fori_loop(0, 2 * D // 256, kv_split, 0)

    @pl.when((far != 0) & jnp.logical_not(is_relay))
    def _():
        for piece in range(PIECES):
            arrived(core, piece)
            mate_copy(block, core, piece).start()

    @pl.when(far != 0)
    def _():
        for piece in range(PIECES):
            arrived(1 - core, piece)
        for piece in range(PIECES):
            mate_copy(block, core, piece).wait_send()

    @pl.when((far == 0) & jnp.logical_not(is_source))
    def _():
        for piece in range(PIECES):
            for half in range(2):
                arrived(half, piece)

    @pl.when(is_relay)
    def _():
        for piece in range(PIECES):
            onward_copy(0, piece).wait_send()

            @pl.when(is_long)
            def _():
                onward_copy(1, piece).wait_send()

    @pl.when(is_source)
    def _():
        for piece in range(PIECES):
            for half in range(2):
                for place in range(4):
                    source_copy(place, half, piece).wait_send()
                mate_copy(modulated, half, piece).wait_send()

    block_both = stacked(block[...].reshape(TOK, D))

    def key_step(step, _):
        columns = pl.ds(pl.multiple_of(step * 256, 256), 256)
        high, low = split(dot_split(block_both, kv_high[:, columns], kv_low[:, columns]))
        k_high[:, columns] = high
        k_low[:, columns] = low
        return 0

    lax.fori_loop(0, D // 256, key_step, 0, unroll=True)

    def value_step(step, _):
        columns = pl.ds(pl.multiple_of(step * 256, 256), 256)
        source = pl.ds(pl.multiple_of(D + step * 256, 256), 256)
        v_t[columns, :] = dot_split(block_both, kv_high[:, source], kv_low[:, source]).T
        return 0

    lax.fori_loop(0, D // 256, value_step, 0, unroll=True)

    ones_rows = jnp.where(lax.broadcasted_iota(jnp.int32, (16, TOK), 0) == 0, 1.0, 0.0)
    tail_row = lax.broadcasted_iota(jnp.int32, (8, TOK), 0)

    def one_head(head):
        keys = pl.ds(pl.multiple_of(window_of(head) * 128, 128), 256)
        keys_high, keys_low = k_high[:, keys], k_low[:, keys]
        queries = q_high[head]
        scores = (
            mul(keys_high, queries)
            + mul(keys_low, queries)
            + mul(keys_high, q_low[head])
            + scores_bias[head]
        )
        top = jnp.max(scores, axis=0, keepdims=True)
        weights_high, weights_low = split(jnp.exp(scores - top))
        values = v_t[pl.ds(pl.multiple_of(head * HEAD_DIM, 16), HEAD_DIM), :]
        values_high, values_low = split(jnp.concatenate([values, ones_rows], axis=0))
        sums = (
            mul(values_high, weights_high)
            + mul(values_low, weights_high)
            + mul(values_high, weights_low)
        )
        tail = jnp.where(tail_row == 1, top, sums[HEAD_DIM:MSG_ROWS])
        return sums[:HEAD_DIM], tail

    def pair_copy(place):
        return pltpu.make_async_remote_copy(
            src_ref=parts_out.at[2 * place + 1 - col_x],
            dst_ref=parts_pair.at[place],
            send_sem=pair_send.at[place],
            recv_sem=pair_recv.at[place],
            device_id=partner,
            device_id_type=MESH,
        )

    def part_copy(place, source):
        return pltpu.make_async_remote_copy(
            src_ref=parts_out.at[2 * place + col_x],
            dst_ref=parts_in.at[source],
            send_sem=part_send.at[place],
            recv_sem=part_recv.at[source],
            device_id=(row, 2 * place + col_x, seed),
            device_id_type=MESH,
        )

    places = [lax.rem(col_y + step, Y) for step in YS] + [col_y]
    for foreign in (True, False):
        for place in places:
            head = 2 * place + (1 - col_x if foreign else col_x)
            sums, tail = one_head(head)
            parts_out[head, :HEAD_DIM] = sums
            parts_out[head, HEAD_DIM:] = tail
            if foreign:
                pair_copy(place).start()

    def merged(place):
        head = 2 * place + col_x
        pair_copy(place).wait_recv()
        mine, theirs = parts_out[head], parts_pair[place]
        top_mine = mine[HEAD_DIM + 1 : HEAD_DIM + 2]
        top_theirs = theirs[HEAD_DIM + 1 : HEAD_DIM + 2]
        top = jnp.maximum(top_mine, top_theirs)
        both = mine * jnp.exp(top_mine - top) + theirs * jnp.exp(top_theirs - top)
        tail = jnp.where(tail_row == 1, top, both[HEAD_DIM:])
        return both[:HEAD_DIM], tail

    for place in places[:-1]:
        head = 2 * place + col_x
        sums, tail = merged(place)
        parts_out[head, :HEAD_DIM] = sums
        parts_out[head, HEAD_DIM:] = tail
        part_copy(place, col_y).start()
    sums, tail = merged(col_y)
    parts_in[col_y, :HEAD_DIM] = sums
    parts_in[col_y, HEAD_DIM:] = tail
    for place in places[-2::-1]:
        part_copy(place, place).wait_recv()
    for place in places:
        pair_copy(place).wait_send()
    for place in places[:-1]:
        part_copy(place, col_y).wait_send()
    tops = parts_in[:, HEAD_DIM + 1 : HEAD_DIM + 2, :]
    factors = jnp.exp(tops - jnp.max(tops, axis=0, keepdims=True))
    total = jnp.sum(factors * parts_in[:, HEAD_DIM : HEAD_DIM + 1, :], axis=0)
    weighted = jnp.sum(factors * parts_in[:, :HEAD_DIM, :], axis=0)
    attended[pl.ds(col, 1)] = (weighted / total)[None]

    def att_copy(place):
        return pltpu.make_async_remote_copy(
            src_ref=attended.at[col],
            dst_ref=attended.at[col],
            send_sem=att_send.at[place],
            recv_sem=att_recv.at[col],
            device_id=(row, 2 * place + col_x, seed),
            device_id_type=MESH,
        )

    def across_copy(head):
        return pltpu.make_async_remote_copy(
            src_ref=attended.at[head],
            dst_ref=attended.at[head],
            send_sem=across_send.at[head // 2],
            recv_sem=att_recv.at[head],
            device_id=partner,
            device_id_type=MESH,
        )

    for place in places[:-1]:
        att_copy(place).start()
    across_copy(col).start()
    loads[13].wait()
    for place in places[-2::-1]:
        head = 2 * place + col_x
        across_copy(head).wait_recv()
        across_copy(head).start()
    for place in places[::-1]:
        across_copy(2 * place + 1 - col_x).wait_recv()
    gated_both = stacked(gates[...] * attended[...].reshape(D, TOK).T)

    def out_step(step, _):
        columns = pl.ds(pl.multiple_of(step * 256, 256), 256)
        high, low = split(out_w[:, columns])
        out_ref[:, columns] = tokens[:, columns] + out_gate[:, columns] * dot_split(
            gated_both, high, low
        )
        return 0

    lax.fori_loop(0, D // 256, out_step, 0, unroll=True)

    for place in places[:-1]:
        att_copy(place).wait_send()
    for place in places:
        across_copy(2 * place + col_x).wait_send()


def body(
    tokens_act,
    single_cond,
    noise_level,
    fourier_freq,
    fourier_phase,
    noise_weight,
    ada_weight,
    query_gate_weight,
    kv_weight,
    out_weight,
    out_gate_weight,
    pair_bias,
    relpos_table,
    chain_id,
    residue_index,
):
    hbm = pl.BlockSpec(memory_space=pltpu.HBM)
    vmem = pltpu.VMEM
    dma = pltpu.SemaphoreType.DMA
    return pl.pallas_call(
        kernel,
        name="attention_block",
        out_shape=jax.ShapeDtypeStruct((TOK, D), F32),
        in_specs=[hbm, hbm, pl.BlockSpec(memory_space=pltpu.SMEM)] + [hbm] * 12,
        out_specs=pl.BlockSpec(memory_space=pltpu.VMEM),
        scratch_shapes=[
            vmem((TOK, D), F32),
            vmem((TOK, C_S), F32),
            vmem((2, 128), F32),
            vmem((2, 128), F32),
            vmem((256, C_S), F32),
            vmem((C_S, 2 * D), F32),
            vmem((D, 2 * D), F32),
            vmem((D, 2 * D), F32),
            vmem((D, D), F32),
            vmem((C_S, D), F32),
            vmem((HEADS, TOK, TOK), BF16),
            vmem((HEADS, 2 * REL + 2), F32),
            vmem((N_ROW, TOK), jnp.int32),
            vmem((N_ROW, TOK), jnp.int32),
            vmem((TOK, 2 * D), F32),
            vmem((2, PIECES, PIECE_ROWS, D), F32),
            vmem((2, PIECES, PIECE_ROWS, D), F32),
            vmem((HEADS, 256, TOK), BF16),
            vmem((HEADS, 256, TOK), BF16),
            vmem((TOK, D), F32),
            vmem((TOK, D), F32),
            vmem((D, TOK), F32),
            vmem((D, TOK), F32),
            vmem((TOK, D), BF16),
            vmem((TOK, D), BF16),
            vmem((D, 2 * D), BF16),
            vmem((D, 2 * D), BF16),
            vmem((HEADS, TOK, TOK), F32),
            vmem((HEADS, MSG_ROWS, TOK), F32),
            vmem((Y, MSG_ROWS, TOK), F32),
            vmem((Y, MSG_ROWS, TOK), F32),
            vmem((HEADS, HEAD_DIM, TOK), F32),
            dma((14,)),
            dma((4, 2, PIECES)),
            dma((2, PIECES)),
            dma((2, PIECES)),
            dma((2, PIECES)),
            dma((Y,)),
            dma((Y,)),
            dma((Y,)),
            dma((Y,)),
            dma((Y,)),
            dma((Y,)),
            dma((N_COL,)),
        ],
        compiler_params=pltpu.CompilerParams(
            collective_id=0, has_side_effects=True, vmem_limit_bytes=60 * 1024 * 1024
        ),
    )(
        tokens_act,
        single_cond,
        noise_level.reshape(1, 1),
        fourier_freq.reshape(2, 128),
        fourier_phase.reshape(2, 128),
        noise_weight,
        ada_weight,
        query_gate_weight,
        kv_weight,
        out_weight,
        out_gate_weight,
        pair_bias,
        relpos_table,
        chain_id.reshape(N_ROW, TOK),
        residue_index.reshape(N_ROW, TOK),
    )


def solution(mesh):
    in_specs = (
        P(("seed", "row"), None),
        P(("seed", "row"), None),
        P("seed"),
        P(),
        P(),
        P(),
        P(),
        P(),
        P(),
        P(),
        P(),
        P(None, "row", "col"),
        P(),
        P(),
        P(),
    )
    out_specs = P(("seed", "row"), None)
    return jax.shard_map(body, mesh=mesh, in_specs=in_specs, out_specs=out_specs, check_vma=False)
```

```python
import jax
import jax.numpy as jnp
from jax import lax
from jax.experimental import pallas as pl
from jax.experimental.pallas import tpu as pltpu
from jax.sharding import PartitionSpec as P

D = 768
HEADS = 16
HEAD_DIM = 48
C_S = 384
REL = 32
TOK = 128
N_ROW = 16
N_COL = 16
Z = 8
Y = 8
YS = (4, 3, 5, 2, 6, 1, 7)
PIECES = 4
PIECE_ROWS = TOK // 2 // PIECES
MSG_ROWS = 56
MESH = pl.DeviceIdType.MESH
F32 = jnp.float32
BF16 = jnp.bfloat16


def split(value):
    high = value.astype(BF16)
    low = (value - high.astype(F32)).astype(BF16)
    return high, low


def mul(left, right):
    return jnp.dot(left, right, preferred_element_type=F32)


def stacked(value):
    high, low = split(value)
    return jnp.concatenate([high, low], axis=0)


def dot_split(both, right_high, right_low):
    rows = both.shape[0] // 2
    first = mul(both, right_high)
    return first[:rows] + first[rows:] + mul(both[:rows], right_low)


def layer_norm(inputs):
    average = jnp.mean(inputs, axis=-1, keepdims=True)
    centred = inputs - average
    variance = jnp.mean(centred * centred, axis=-1, keepdims=True)
    return centred * lax.rsqrt(variance + 1e-05)


def sigmoid(value):
    return 1.0 / (1.0 + jnp.exp(-value))


def kernel(
    tokens_hbm,
    cond_hbm,
    noise_ref,
    freq_hbm,
    phase_hbm,
    noise_w_hbm,
    ada_w_hbm,
    qg_w_hbm,
    kv_w_hbm,
    out_w_hbm,
    og_w_hbm,
    bias_hbm,
    table_hbm,
    chain_hbm,
    residue_hbm,
    out_hbm,
    tokens,
    cond,
    freq,
    phase,
    noise_w,
    ada_w,
    qg_w,
    kv_w,
    out_w,
    og_w,
    bias,
    table,
    chain,
    residue,
    ada,
    modulated,
    block,
    q_high,
    q_low,
    gates,
    out_gate,
    q_t,
    v_t,
    k_high,
    k_low,
    kv_high,
    kv_low,
    scores_bias,
    parts_out,
    parts_in,
    parts_pair,
    attended,
    result,
    load_sems,
    store_sems,
    source_send,
    onward_send,
    mate_send,
    block_recv,
    pair_send,
    pair_recv,
    part_send,
    part_recv,
    att_send,
    across_send,
    att_recv,
):
    row = lax.axis_index("row")
    col = lax.axis_index("col")
    seed = lax.axis_index("seed")
    z, core = row // 2, lax.rem(row, 2)
    mate = (row + 1 - 2 * core, col, seed)
    col_y, col_x = col // 2, lax.rem(col, 2)
    partner = (row, 2 * col_y + 1 - col_x, seed)
    is_source = row == col
    far = lax.rem(z + Z - col // 2, Z)
    is_relay = (far == 2) | (far == 6)
    onward = jnp.where(far == 2, 1, -1)
    is_long = is_relay & ((far == 2) == (core == 0))
    long_first = col // 2 == 4
    first_place = jnp.where(long_first, 1, 0)

    def along(delta, which):
        return (2 * lax.rem(z + Z + delta, Z) + which, col, seed)

    pairs = (
        (freq_hbm, freq),
        (phase_hbm, phase),
        (noise_w_hbm, noise_w),
        (cond_hbm, cond),
        (tokens_hbm, tokens),
        (ada_w_hbm, ada_w),
        (qg_w_hbm, qg_w),
        (chain_hbm, chain),
        (residue_hbm, residue),
        (table_hbm, table),
        (bias_hbm, bias),
        (og_w_hbm, og_w),
        (kv_w_hbm, kv_w),
        (out_w_hbm, out_w),
    )
    loads = {
        number: pltpu.make_async_copy(source, target, load_sems.at[number])
        for number, (source, target) in enumerate(pairs)
    }
    for number in range(6):
        loads[number].start()

    barrier = pltpu.get_barrier_semaphore()

    def greet(step, _):
        pl.semaphore_signal(
            barrier,
            inc=1,
            device_id=(row, lax.rem(col + 2 * step, N_COL), seed),
            device_id_type=MESH,
        )
        return 0

    sender_delta = jnp.where(
        far == 3, -1, jnp.where(far == 5, 1, jnp.where(core == 0, -2, 2))
    )
    is_onward = (far >= 3) & (far <= 5)
    sender = jnp.where(is_onward, along(sender_delta, core)[0], col)

    @pl.when(far != 0)
    def _():
        pl.semaphore_signal(
            barrier, inc=1, device_id=(sender, col, seed), device_id_type=MESH
        )

    pl.semaphore_signal(barrier, inc=1, device_id=mate, device_id_type=MESH)
    pl.semaphore_signal(barrier, inc=1, device_id=partner, device_id_type=MESH)
    lax.fori_loop(1, Y, greet, 0)
    expected = (
        Y
        + 1
        + jnp.where(is_source, 8, 0)
        + jnp.where(is_relay, 1, 0)
        + jnp.where(is_long, 1, 0)
    )

    for number in (0, 1):
        loads[number].wait()
    level = jnp.full((2, 128), noise_ref[0, 0], F32)
    noise_scaled = 0.25 * jnp.log(level / 16.0)
    features = jnp.cos(2.0 * jnp.pi * (noise_scaled * freq[...] + phase[...]))
    feature_row = layer_norm(jnp.concatenate([features[0:1], features[1:2]], axis=1))
    feature_rows = jnp.broadcast_to(feature_row, (16, 256))
    loads[2].wait()
    noise_high, noise_low = split(noise_w[...])
    shift = dot_split(stacked(feature_rows), noise_high, noise_low)[0:1]
    loads[3].wait()
    cond_both = stacked(layer_norm(cond[...] + shift))
    loads[4].wait()
    tokens_norm = layer_norm(tokens[...])
    loads[5].wait()
    for number in range(6, len(pairs)):
        loads[number].start()

    def ada_step(step, _):
        columns = pl.ds(pl.multiple_of(step * 256, 256), 256)
        high, low = split(ada_w[:, columns])
        ada[:, columns] = dot_split(cond_both, high, low)
        return 0

    lax.fori_loop(0, 2 * D // 256, ada_step, 0, unroll=True)
    modulated[...] = (sigmoid(ada[:, :D]) * tokens_norm + ada[:, D:]).reshape(2, PIECES, PIECE_ROWS, D)

    pl.semaphore_wait(barrier, expected)

    def source_copy(place, half, piece):
        return pltpu.make_async_remote_copy(
            src_ref=modulated.at[half, piece],
            dst_ref=block.at[half, piece],
            send_sem=source_send.at[place, half, piece],
            recv_sem=block_recv.at[half, piece],
            device_id=along((2, -2, 1, -1)[place], half),
            device_id_type=MESH,
        )

    def onward_copy(place, piece):
        return pltpu.make_async_remote_copy(
            src_ref=block.at[core, piece],
            dst_ref=block.at[core, piece],
            send_sem=onward_send.at[place, piece],
            recv_sem=block_recv.at[core, piece],
            device_id=along(onward * (place + 1), core),
            device_id_type=MESH,
        )

    def mate_copy(source, half, piece):
        return pltpu.make_async_remote_copy(
            src_ref=source.at[half, piece],
            dst_ref=block.at[half, piece],
            send_sem=mate_send.at[half, piece],
            recv_sem=block_recv.at[half, piece],
            device_id=mate,
            device_id_type=MESH,
        )

    def arrived(half, piece):
        mate_copy(block, half, piece).wait_recv()

    @pl.when(is_source)
    def _():
        for places in ((0, 1), (2, 3)):
            for piece in range(PIECES):
                for place in places:
                    for half in range(2):
                        source_copy(place, half, piece).start()
            if places[0] == 0:
                for piece in range(PIECES):
                    for half in range(2):
                        mate_copy(modulated, half, piece).start()
        block[...] = modulated[...]

    @pl.when(is_relay)
    def _():
        for piece in range(PIECES):
            arrived(core, piece)

            @pl.when(is_long | jnp.logical_not(long_first))
            def _():
                onward_copy(first_place, piece).start()

            mate_copy(block, core, piece).start()
        for piece in range(PIECES):

            @pl.when(is_long | long_first)
            def _():
                onward_copy(1 - first_place, piece).start()

    mod_both = stacked(modulated[...].reshape(TOK, D))
    loads[6].wait()

    def query_step(step, _):
        columns = pl.ds(pl.multiple_of(step * 256, 256), 256)
        high, low = split(qg_w[:, columns])
        result = dot_split(mod_both, high, low) * (HEAD_DIM**-0.5)
        q_t[columns, :] = result.T
        return 0

    lax.fori_loop(0, D // 256, query_step, 0, unroll=True)

    def gate_step(step, _):
        columns = pl.ds(pl.multiple_of(step * 256, 256), 256)
        high, low = split(qg_w[:, pl.ds(pl.multiple_of(D + step * 256, 256), 256)])
        gates[:, columns] = sigmoid(dot_split(mod_both, high, low))
        return 0

    lax.fori_loop(0, D // 256, gate_step, 0, unroll=True)
    window_row = lax.broadcasted_iota(jnp.int32, (256, TOK), 0)

    def window_of(half, two):
        return pl.multiple_of((3 * half + two // 2) * 128, 128)

    def query_mask(number, _):
        start = window_of(number // 4, lax.rem(number, 4))
        window = q_t[pl.ds(start, 256), :]
        for member in range(2):
            place = (2 * number + member) * HEAD_DIM - start
            inside = (window_row >= place) & (window_row < place + HEAD_DIM)
            high, low = split(jnp.where(inside, window, 0.0))
            q_high[number, :, member * TOK : (member + 1) * TOK] = high
            q_low[number, :, member * TOK : (member + 1) * TOK] = low
        return 0

    lax.fori_loop(0, HEADS // 2, query_mask, 0)

    for number in (7, 8, 9, 10):
        loads[number].wait()
    chain_f = chain[...].astype(F32)
    residue_f = residue[...].astype(F32)
    place = lax.broadcasted_iota(jnp.int32, (N_ROW, TOK), 0)

    def pick(values, which):
        chosen = jnp.sum(jnp.where(place == which, values, 0.0), axis=0, keepdims=True)
        return jnp.broadcast_to(chosen, (TOK, TOK))

    same = pick(chain_f, row) == pick(chain_f, col).T
    offset = jnp.clip(pick(residue_f, row) - pick(residue_f, col).T, -REL, REL) + REL
    bucket = jnp.where(same, offset, 2.0 * REL + 1.0).astype(jnp.int32)
    wide = jnp.concatenate(
        [table[...], jnp.zeros((HEADS, 128 - 2 * REL - 2), F32)], axis=1
    )
    table_rows = [wide[head : head + 1] for head in range(HEADS)]
    for head in range(HEADS):
        rel = jnp.take_along_axis(
            jnp.broadcast_to(table_rows[head], (TOK, 128)), bucket, axis=1
        )
        scores_bias[head] = bias[head].astype(F32).T + rel

    loads[11].wait()

    def out_gate_step(step, _):
        columns = pl.ds(pl.multiple_of(step * 256, 256), 256)
        high, low = split(og_w[:, columns])
        out_gate[:, columns] = sigmoid(dot_split(cond_both, high, low))
        return 0

    lax.fori_loop(0, D // 256, out_gate_step, 0, unroll=True)
    loads[12].wait()

    def kv_split(part, _):
        half, kind = part // 2, lax.rem(part, 2)
        for tile in range(3):
            source = pl.multiple_of(kind * D + half * 384 + tile * 128, 128)
            target = pl.multiple_of(half * D + kind * 384 + tile * 128, 128)
            high, low = split(kv_w[:, pl.ds(source, 128)])
            kv_high[:, pl.ds(target, 128)] = high
            kv_low[:, pl.ds(target, 128)] = low
        return 0

    lax.fori_loop(0, 4, kv_split, 0)

    @pl.when((far != 0) & jnp.logical_not(is_relay))
    def _():
        for piece in range(PIECES):
            arrived(core, piece)
            mate_copy(block, core, piece).start()

    @pl.when(far != 0)
    def _():
        for piece in range(PIECES):
            arrived(1 - core, piece)
        for piece in range(PIECES):
            mate_copy(block, core, piece).wait_send()

    @pl.when((far == 0) & jnp.logical_not(is_source))
    def _():
        for piece in range(PIECES):
            for half in range(2):
                arrived(half, piece)

    @pl.when(is_relay)
    def _():
        for piece in range(PIECES):
            onward_copy(0, piece).wait_send()

            @pl.when(is_long)
            def _():
                onward_copy(1, piece).wait_send()

    @pl.when(is_source)
    def _():
        for piece in range(PIECES):
            for half in range(2):
                for place in range(4):
                    source_copy(place, half, piece).wait_send()
                mate_copy(modulated, half, piece).wait_send()

    block_both = stacked(block[...].reshape(TOK, D))

    def keys_values(half):
        for step in range(3):
            columns = pl.ds(pl.multiple_of(half * D + step * 256, 128), 256)
            both = dot_split(block_both, kv_high[:, columns], kv_low[:, columns])
            for tile in range(2):
                place = 2 * step + tile
                part = both[:, tile * 128 : (tile + 1) * 128]
                target = pl.ds(pl.multiple_of(half * 384 + place % 3 * 128, 128), 128)
                if place < 3:
                    high, low = split(part)
                    k_high[:, target] = high
                    k_low[:, target] = low
                else:
                    v_t[target, :] = part.T

    ones_rows = jnp.where(lax.broadcasted_iota(jnp.int32, (16, TOK), 0) == 0, 1.0, 0.0)
    tail_row = lax.broadcasted_iota(jnp.int32, (8, TOK), 0)

    none = jnp.zeros((64, TOK), BF16)

    def two_heads(half, two):
        number = 4 * half + two
        keys = pl.ds(window_of(half, two), 256)
        keys_high = k_high[:, keys]
        queries_low = mul(keys_high, q_low[number])
        both = mul(jnp.concatenate([keys_high, k_low[:, keys]], axis=0), q_high[number])
        products = both[:TOK] + both[TOK:] + queries_low
        tops, highs, lows, values = [], [], [], []
        for member in range(2):
            head = 2 * number + member
            scores = products[:, member * TOK : (member + 1) * TOK] + scores_bias[head]
            top = jnp.max(scores, axis=0, keepdims=True)
            high, low = split(jnp.exp(scores - top))
            tops.append(top)
            highs.append(high)
            lows.append(low)
            value = v_t[pl.ds(pl.multiple_of(head * HEAD_DIM, 16), HEAD_DIM), :]
            high, low = split(jnp.concatenate([value, ones_rows], axis=0))
            values.append(jnp.concatenate([high, high], axis=1))
            values.append(jnp.concatenate([low, none], axis=1))
        weights = jnp.concatenate(
            [jnp.concatenate(highs, axis=1), jnp.concatenate(lows, axis=1)], axis=0
        )
        sums = mul(jnp.concatenate(values, axis=0), weights)
        for member in range(2):
            head = 2 * number + member
            columns = slice(member * TOK, (member + 1) * TOK)
            result = (
                sums[128 * member : 128 * member + 64, columns]
                + sums[128 * member + 64 : 128 * member + 128, columns]
            )
            parts_out[head, :HEAD_DIM] = result[:HEAD_DIM]
            parts_out[head, HEAD_DIM:] = jnp.where(
                tail_row == 1, tops[member], result[HEAD_DIM:MSG_ROWS]
            )

    def pair_copy(place):
        return pltpu.make_async_remote_copy(
            src_ref=parts_out.at[8 * (1 - col_x) + place],
            dst_ref=parts_pair.at[place],
            send_sem=pair_send.at[place],
            recv_sem=pair_recv.at[place],
            device_id=partner,
            device_id_type=MESH,
        )

    def part_copy(place, source):
        return pltpu.make_async_remote_copy(
            src_ref=parts_out.at[8 * col_x + place],
            dst_ref=parts_in.at[source],
            send_sem=part_send.at[place],
            recv_sem=part_recv.at[source],
            device_id=(row, 2 * place + col_x, seed),
            device_id_type=MESH,
        )

    places = [lax.rem(col_y + step, Y) for step in YS] + [col_y]
    twos = [lax.rem(col_y // 2 + step, 4) for step in (2, 1, 3, 0)]
    keys_values(1 - col_x)
    for two in twos:
        two_heads(1 - col_x, two)
        for member in range(2):
            pair_copy(2 * two + member).start()
    keys_values(col_x)
    for two in twos:
        two_heads(col_x, two)

    def merged(place):
        head = 8 * col_x + place
        pair_copy(place).wait_recv()
        mine, theirs = parts_out[head], parts_pair[place]
        top_mine = mine[HEAD_DIM + 1 : HEAD_DIM + 2]
        top_theirs = theirs[HEAD_DIM + 1 : HEAD_DIM + 2]
        top = jnp.maximum(top_mine, top_theirs)
        both = mine * jnp.exp(top_mine - top) + theirs * jnp.exp(top_theirs - top)
        tail = jnp.where(tail_row == 1, top, both[HEAD_DIM:])
        return both[:HEAD_DIM], tail

    for place in places[:-1]:
        head = 8 * col_x + place
        sums, tail = merged(place)
        parts_out[head, :HEAD_DIM] = sums
        parts_out[head, HEAD_DIM:] = tail
        part_copy(place, col_y).start()
    sums, tail = merged(col_y)
    parts_in[col_y, :HEAD_DIM] = sums
    parts_in[col_y, HEAD_DIM:] = tail
    for place in places[-2::-1]:
        part_copy(place, place).wait_recv()
    for place in places:
        pair_copy(place).wait_send()
    for place in places[:-1]:
        part_copy(place, col_y).wait_send()
    tops = parts_in[:, HEAD_DIM + 1 : HEAD_DIM + 2, :]
    factors = jnp.exp(tops - jnp.max(tops, axis=0, keepdims=True))
    total = jnp.sum(factors * parts_in[:, HEAD_DIM : HEAD_DIM + 1, :], axis=0)
    weighted = jnp.sum(factors * parts_in[:, :HEAD_DIM, :], axis=0)
    own = 8 * col_x + col_y
    attended[pl.ds(own, 1)] = (weighted / total)[None]

    def att_copy(place):
        return pltpu.make_async_remote_copy(
            src_ref=attended.at[own],
            dst_ref=attended.at[own],
            send_sem=att_send.at[place],
            recv_sem=att_recv.at[own],
            device_id=(row, 2 * place + col_x, seed),
            device_id_type=MESH,
        )

    def across_copy(head):
        return pltpu.make_async_remote_copy(
            src_ref=attended.at[head],
            dst_ref=attended.at[head],
            send_sem=across_send.at[lax.rem(head, 8)],
            recv_sem=att_recv.at[head],
            device_id=partner,
            device_id_type=MESH,
        )

    for place in places[:-1]:
        att_copy(place).start()
    across_copy(own).start()
    loads[13].wait()
    for place in places[-2::-1]:
        head = 8 * col_x + place
        across_copy(head).wait_recv()
        across_copy(head).start()

    def projected(half):
        rows = pl.ds(pl.multiple_of(half * 384, 128), 384)
        results = attended[pl.ds(8 * half, 8)].reshape(384, TOK).T
        gated_both = stacked(gates[:, rows] * results)
        terms = []
        for step in range(D // 256):
            high, low = split(out_w[rows, step * 256 : (step + 1) * 256])
            terms.append(dot_split(gated_both, high, low))
        return terms

    for step, term in enumerate(projected(col_x)):
        ada[:, step * 256 : (step + 1) * 256] = term
    for place in places[::-1]:
        across_copy(8 * (1 - col_x) + place).wait_recv()
    stores = []
    for step, term in enumerate(projected(1 - col_x)):
        columns = slice(step * 256, (step + 1) * 256)
        result[:, columns] = tokens[:, columns] + out_gate[:, columns] * (
            term + ada[:, columns]
        )
        store = pltpu.make_async_copy(
            result.at[:, columns], out_hbm.at[:, columns], store_sems.at[step]
        )
        store.start()
        stores.append(store)

    for place in places[:-1]:
        att_copy(place).wait_send()
    for place in places:
        across_copy(8 * col_x + place).wait_send()
    for store in stores:
        store.wait()


def body(
    tokens_act,
    single_cond,
    noise_level,
    fourier_freq,
    fourier_phase,
    noise_weight,
    ada_weight,
    query_gate_weight,
    kv_weight,
    out_weight,
    out_gate_weight,
    pair_bias,
    relpos_table,
    chain_id,
    residue_index,
):
    hbm = pl.BlockSpec(memory_space=pltpu.HBM)
    vmem = pltpu.VMEM
    dma = pltpu.SemaphoreType.DMA
    return pl.pallas_call(
        kernel,
        name="attention_block",
        out_shape=jax.ShapeDtypeStruct((TOK, D), F32),
        in_specs=[hbm, hbm, pl.BlockSpec(memory_space=pltpu.SMEM)] + [hbm] * 12,
        out_specs=hbm,
        scratch_shapes=[
            vmem((TOK, D), F32),
            vmem((TOK, C_S), F32),
            vmem((2, 128), F32),
            vmem((2, 128), F32),
            vmem((256, C_S), F32),
            vmem((C_S, 2 * D), F32),
            vmem((D, 2 * D), F32),
            vmem((D, 2 * D), F32),
            vmem((D, D), F32),
            vmem((C_S, D), F32),
            vmem((HEADS, TOK, TOK), BF16),
            vmem((HEADS, 2 * REL + 2), F32),
            vmem((N_ROW, TOK), jnp.int32),
            vmem((N_ROW, TOK), jnp.int32),
            vmem((TOK, 2 * D), F32),
            vmem((2, PIECES, PIECE_ROWS, D), F32),
            vmem((2, PIECES, PIECE_ROWS, D), F32),
            vmem((HEADS // 2, 256, 2 * TOK), BF16),
            vmem((HEADS // 2, 256, 2 * TOK), BF16),
            vmem((TOK, D), F32),
            vmem((TOK, D), F32),
            vmem((D, TOK), F32),
            vmem((D, TOK), F32),
            vmem((TOK, D), BF16),
            vmem((TOK, D), BF16),
            vmem((D, 2 * D), BF16),
            vmem((D, 2 * D), BF16),
            vmem((HEADS, TOK, TOK), F32),
            vmem((HEADS, MSG_ROWS, TOK), F32),
            vmem((Y, MSG_ROWS, TOK), F32),
            vmem((Y, MSG_ROWS, TOK), F32),
            vmem((HEADS, HEAD_DIM, TOK), F32),
            vmem((TOK, D), F32),
            dma((14,)),
            dma((3,)),
            dma((4, 2, PIECES)),
            dma((2, PIECES)),
            dma((2, PIECES)),
            dma((2, PIECES)),
            dma((Y,)),
            dma((Y,)),
            dma((Y,)),
            dma((Y,)),
            dma((Y,)),
            dma((Y,)),
            dma((N_COL,)),
        ],
        compiler_params=pltpu.CompilerParams(
            collective_id=0, has_side_effects=True, vmem_limit_bytes=60 * 1024 * 1024
        ),
    )(
        tokens_act,
        single_cond,
        noise_level.reshape(1, 1),
        fourier_freq.reshape(2, 128),
        fourier_phase.reshape(2, 128),
        noise_weight,
        ada_weight,
        query_gate_weight,
        kv_weight,
        out_weight,
        out_gate_weight,
        pair_bias,
        relpos_table,
        chain_id.reshape(N_ROW, TOK),
        residue_index.reshape(N_ROW, TOK),
    )


def solution(mesh):
    in_specs = (
        P(("seed", "row"), None),
        P(("seed", "row"), None),
        P("seed"),
        P(),
        P(),
        P(),
        P(),
        P(),
        P(),
        P(),
        P(),
        P(None, "row", "col"),
        P(),
        P(),
        P(),
    )
    out_specs = P(("seed", "row"), None)
    return jax.shard_map(body, mesh=mesh, in_specs=in_specs, out_specs=out_specs, check_vma=False)
```

```python
import jax
import jax.numpy as jnp
from jax import lax
from jax.experimental import pallas as pl
from jax.experimental.pallas import tpu as pltpu
from jax.sharding import PartitionSpec as P

D = 768
HEADS = 16
HEAD_DIM = 48
C_S = 384
REL = 32
TOK = 128
N_ROW = 16
N_COL = 16
Z = 8
Y = 8
YS = (4, 3, 5, 2, 6, 1, 7)
PIECES = 4
PIECE_ROWS = TOK // 2 // PIECES
MSG_ROWS = 56
MESH = pl.DeviceIdType.MESH
F32 = jnp.float32
BF16 = jnp.bfloat16


def split(value):
    high = value.astype(BF16)
    low = (value - high.astype(F32)).astype(BF16)
    return high, low


def mul(left, right):
    return jnp.dot(left, right, preferred_element_type=F32)


def stacked(value):
    high, low = split(value)
    return jnp.concatenate([high, low], axis=0)


def dot_split(both, right_high, right_low):
    rows = both.shape[0] // 2
    first = mul(both, right_high)
    return first[:rows] + first[rows:] + mul(both[:rows], right_low)


def layer_norm(inputs):
    average = jnp.mean(inputs, axis=-1, keepdims=True)
    centred = inputs - average
    variance = jnp.mean(centred * centred, axis=-1, keepdims=True)
    return centred * lax.rsqrt(variance + 1e-05)


def sigmoid(value):
    return 1.0 / (1.0 + jnp.exp(-value))


def kernel(
    tokens_hbm,
    cond_hbm,
    noise_ref,
    freq_hbm,
    phase_hbm,
    noise_w_hbm,
    ada_w_hbm,
    qg_w_hbm,
    kv_w_hbm,
    out_w_hbm,
    og_w_hbm,
    bias_hbm,
    table_hbm,
    chain_hbm,
    residue_hbm,
    out_hbm,
    tokens,
    cond,
    freq,
    phase,
    noise_w,
    ada_w,
    qg_w,
    kv_w,
    out_w,
    og_w,
    bias,
    table,
    chain,
    residue,
    ada,
    modulated,
    block,
    q_high,
    q_low,
    gates,
    out_gate,
    q_t,
    v_t,
    k_high,
    k_low,
    kv_high,
    kv_low,
    scores_bias,
    parts_out,
    parts_in,
    parts_pair,
    attended,
    result,
    load_sems,
    store_sems,
    source_send,
    onward_send,
    mate_send,
    block_recv,
    pair_send,
    pair_recv,
    part_send,
    part_recv,
    att_send,
    across_send,
    att_recv,
):
    row = lax.axis_index("row")
    col = lax.axis_index("col")
    seed = lax.axis_index("seed")
    z, core = row // 2, lax.rem(row, 2)
    mate = (row + 1 - 2 * core, col, seed)
    col_y, col_x = col // 2, lax.rem(col, 2)
    partner = (row, 2 * col_y + 1 - col_x, seed)
    is_source = row == col
    far = lax.rem(z + Z - col // 2, Z)
    is_relay = (far == 2) | (far == 6)
    onward = jnp.where(far == 2, 1, -1)
    is_long = is_relay & ((far == 2) == (core == 0))
    long_first = col // 2 == 4
    first_place = jnp.where(long_first, 1, 0)

    def along(delta, which):
        return (2 * lax.rem(z + Z + delta, Z) + which, col, seed)

    pairs = (
        (freq_hbm, freq),
        (phase_hbm, phase),
        (noise_w_hbm, noise_w),
        (cond_hbm, cond),
        (tokens_hbm, tokens),
        (ada_w_hbm, ada_w),
        (qg_w_hbm, qg_w),
        (chain_hbm, chain),
        (residue_hbm, residue),
        (table_hbm, table),
        (bias_hbm, bias),
        (og_w_hbm, og_w),
        (kv_w_hbm, kv_w),
        (out_w_hbm, out_w),
    )
    loads = {
        number: pltpu.make_async_copy(source, target, load_sems.at[number])
        for number, (source, target) in enumerate(pairs)
    }
    for number in range(6):
        loads[number].start()

    barrier = pltpu.get_barrier_semaphore()

    def greet(step, _):
        pl.semaphore_signal(
            barrier,
            inc=1,
            device_id=(row, lax.rem(col + 2 * step, N_COL), seed),
            device_id_type=MESH,
        )
        return 0

    sender_delta = jnp.where(
        far == 3, -1, jnp.where(far == 5, 1, jnp.where(core == 0, -2, 2))
    )
    is_onward = (far >= 3) & (far <= 5)
    sender = jnp.where(is_onward, along(sender_delta, core)[0], col)

    @pl.when(far != 0)
    def _():
        pl.semaphore_signal(
            barrier, inc=1, device_id=(sender, col, seed), device_id_type=MESH
        )

    pl.semaphore_signal(barrier, inc=1, device_id=mate, device_id_type=MESH)
    pl.semaphore_signal(barrier, inc=1, device_id=partner, device_id_type=MESH)
    lax.fori_loop(1, Y, greet, 0)
    expected = (
        Y
        + 1
        + jnp.where(is_source, 8, 0)
        + jnp.where(is_relay, 1, 0)
        + jnp.where(is_long, 1, 0)
    )

    for number in (0, 1):
        loads[number].wait()
    level = jnp.full((2, 128), noise_ref[0, 0], F32)
    noise_scaled = 0.25 * jnp.log(level / 16.0)
    features = jnp.cos(2.0 * jnp.pi * (noise_scaled * freq[...] + phase[...]))
    feature_row = layer_norm(jnp.concatenate([features[0:1], features[1:2]], axis=1))
    feature_rows = jnp.broadcast_to(feature_row, (16, 256))
    loads[2].wait()
    noise_high, noise_low = split(noise_w[...])
    shift = dot_split(stacked(feature_rows), noise_high, noise_low)[0:1]
    loads[3].wait()
    cond_both = stacked(layer_norm(cond[...] + shift))
    loads[4].wait()
    tokens_norm = layer_norm(tokens[...])
    loads[5].wait()
    for number in range(6, len(pairs)):
        loads[number].start()

    def ada_step(step, _):
        columns = pl.ds(pl.multiple_of(step * 256, 256), 256)
        high, low = split(ada_w[:, columns])
        ada[:, columns] = dot_split(cond_both, high, low)
        return 0

    lax.fori_loop(0, 2 * D // 256, ada_step, 0, unroll=True)
    modulated[...] = (sigmoid(ada[:, :D]) * tokens_norm + ada[:, D:]).reshape(2, PIECES, PIECE_ROWS, D)

    pl.semaphore_wait(barrier, expected)

    def source_copy(place, half, piece):
        return pltpu.make_async_remote_copy(
            src_ref=modulated.at[half, piece],
            dst_ref=block.at[half, piece],
            send_sem=source_send.at[place, half, piece],
            recv_sem=block_recv.at[half, piece],
            device_id=along((2, -2, 1, -1)[place], half),
            device_id_type=MESH,
        )

    def onward_copy(place, piece):
        return pltpu.make_async_remote_copy(
            src_ref=block.at[core, piece],
            dst_ref=block.at[core, piece],
            send_sem=onward_send.at[place, piece],
            recv_sem=block_recv.at[core, piece],
            device_id=along(onward * (place + 1), core),
            device_id_type=MESH,
        )

    def mate_copy(source, half, piece):
        return pltpu.make_async_remote_copy(
            src_ref=source.at[half, piece],
            dst_ref=block.at[half, piece],
            send_sem=mate_send.at[half, piece],
            recv_sem=block_recv.at[half, piece],
            device_id=mate,
            device_id_type=MESH,
        )

    def arrived(half, piece):
        mate_copy(block, half, piece).wait_recv()

    @pl.when(is_source)
    def _():
        for places in ((0, 1), (2, 3)):
            for piece in range(PIECES):
                for place in places:
                    for half in range(2):
                        source_copy(place, half, piece).start()
            if places[0] == 0:
                for piece in range(PIECES):
                    for half in range(2):
                        mate_copy(modulated, half, piece).start()
        block[...] = modulated[...]

    @pl.when(is_relay)
    def _():
        for piece in range(PIECES):
            arrived(core, piece)

            @pl.when(is_long | jnp.logical_not(long_first))
            def _():
                onward_copy(first_place, piece).start()

            mate_copy(block, core, piece).start()
        for piece in range(PIECES):

            @pl.when(is_long | long_first)
            def _():
                onward_copy(1 - first_place, piece).start()

    mod_both = stacked(modulated[...].reshape(TOK, D))
    loads[6].wait()

    def query_step(step, _):
        columns = pl.ds(pl.multiple_of(step * 256, 256), 256)
        high, low = split(qg_w[:, columns])
        result = dot_split(mod_both, high, low) * (HEAD_DIM**-0.5)
        q_t[columns, :] = result.T
        return 0

    lax.fori_loop(0, D // 256, query_step, 0, unroll=True)

    def gate_step(step, _):
        columns = pl.ds(pl.multiple_of(step * 256, 256), 256)
        high, low = split(qg_w[:, pl.ds(pl.multiple_of(D + step * 256, 256), 256)])
        gates[:, columns] = sigmoid(dot_split(mod_both, high, low))
        return 0

    lax.fori_loop(0, D // 256, gate_step, 0, unroll=True)
    window_row = lax.broadcasted_iota(jnp.int32, (256, TOK), 0)

    def window_of(half, two):
        return pl.multiple_of((3 * half + two // 2) * 128, 128)

    def query_mask(number, _):
        start = window_of(number // 4, lax.rem(number, 4))
        window = q_t[pl.ds(start, 256), :]
        for member in range(2):
            place = (2 * number + member) * HEAD_DIM - start
            inside = (window_row >= place) & (window_row < place + HEAD_DIM)
            high, low = split(jnp.where(inside, window, 0.0))
            q_high[number, :, member * TOK : (member + 1) * TOK] = high
            q_low[number, :, member * TOK : (member + 1) * TOK] = low
        return 0

    lax.fori_loop(0, HEADS // 2, query_mask, 0)

    for number in (7, 8, 9, 10):
        loads[number].wait()
    chain_f = chain[...].astype(F32)
    residue_f = residue[...].astype(F32)
    place = lax.broadcasted_iota(jnp.int32, (N_ROW, TOK), 0)

    def pick(values, which):
        chosen = jnp.sum(jnp.where(place == which, values, 0.0), axis=0, keepdims=True)
        return jnp.broadcast_to(chosen, (TOK, TOK))

    same = pick(chain_f, row) == pick(chain_f, col).T
    offset = jnp.clip(pick(residue_f, row) - pick(residue_f, col).T, -REL, REL) + REL
    bucket = jnp.where(same, offset, 2.0 * REL + 1.0).astype(jnp.int32)
    wide = jnp.concatenate(
        [table[...], jnp.zeros((HEADS, 128 - 2 * REL - 2), F32)], axis=1
    )
    table_rows = [wide[head : head + 1] for head in range(HEADS)]
    for head in range(HEADS):
        rel = jnp.take_along_axis(
            jnp.broadcast_to(table_rows[head], (TOK, 128)), bucket, axis=1
        )
        scores_bias[head] = bias[head].astype(F32).T + rel

    loads[11].wait()

    def out_gate_step(step, _):
        columns = pl.ds(pl.multiple_of(step * 256, 256), 256)
        high, low = split(og_w[:, columns])
        out_gate[:, columns] = sigmoid(dot_split(cond_both, high, low))
        return 0

    lax.fori_loop(0, D // 256, out_gate_step, 0, unroll=True)
    loads[12].wait()

    def kv_split(part, _):
        half, kind = part // 2, lax.rem(part, 2)
        for tile in range(3):
            source = pl.multiple_of(kind * D + half * 384 + tile * 128, 128)
            target = pl.multiple_of(half * D + kind * 384 + tile * 128, 128)
            high, low = split(kv_w[:, pl.ds(source, 128)])
            kv_high[:, pl.ds(target, 128)] = high
            kv_low[:, pl.ds(target, 128)] = low
        return 0

    lax.fori_loop(0, 4, kv_split, 0)

    @pl.when((far != 0) & jnp.logical_not(is_relay))
    def _():
        for piece in range(PIECES):
            arrived(core, piece)
            mate_copy(block, core, piece).start()

    @pl.when(far != 0)
    def _():
        for piece in range(PIECES):
            arrived(1 - core, piece)
        for piece in range(PIECES):
            mate_copy(block, core, piece).wait_send()

    @pl.when((far == 0) & jnp.logical_not(is_source))
    def _():
        for piece in range(PIECES):
            for half in range(2):
                arrived(half, piece)

    @pl.when(is_relay)
    def _():
        for piece in range(PIECES):
            onward_copy(0, piece).wait_send()

            @pl.when(is_long)
            def _():
                onward_copy(1, piece).wait_send()

    @pl.when(is_source)
    def _():
        for piece in range(PIECES):
            for half in range(2):
                for place in range(4):
                    source_copy(place, half, piece).wait_send()
                mate_copy(modulated, half, piece).wait_send()

    block_both = stacked(block[...].reshape(TOK, D))

    def keys_values(half):
        for step in range(3):
            columns = pl.ds(pl.multiple_of(half * D + step * 256, 128), 256)
            both = dot_split(block_both, kv_high[:, columns], kv_low[:, columns])
            for tile in range(2):
                place = 2 * step + tile
                part = both[:, tile * 128 : (tile + 1) * 128]
                target = pl.ds(pl.multiple_of(half * 384 + place % 3 * 128, 128), 128)
                if place < 3:
                    high, low = split(part)
                    k_high[:, target] = high
                    k_low[:, target] = low
                else:
                    v_t[target, :] = part.T

    ones_rows = jnp.where(lax.broadcasted_iota(jnp.int32, (16, TOK), 0) == 0, 1.0, 0.0)
    tail_row = lax.broadcasted_iota(jnp.int32, (8, TOK), 0)

    none = jnp.zeros((64, TOK), BF16)

    def two_heads(half, two):
        number = 4 * half + two
        keys = pl.ds(window_of(half, two), 256)
        keys_high = k_high[:, keys]
        queries_low = mul(keys_high, q_low[number])
        both = mul(jnp.concatenate([keys_high, k_low[:, keys]], axis=0), q_high[number])
        products = both[:TOK] + both[TOK:] + queries_low
        tops, highs, lows, values = [], [], [], []
        for member in range(2):
            head = 2 * number + member
            scores = products[:, member * TOK : (member + 1) * TOK] + scores_bias[head]
            top = jnp.max(scores, axis=0, keepdims=True)
            high, low = split(jnp.exp(scores - top))
            tops.append(top)
            highs.append(high)
            lows.append(low)
            value = v_t[pl.ds(pl.multiple_of(head * HEAD_DIM, 16), HEAD_DIM), :]
            high, low = split(jnp.concatenate([value, ones_rows], axis=0))
            values.append(jnp.concatenate([high, high], axis=1))
            values.append(jnp.concatenate([low, none], axis=1))
        weights = jnp.concatenate(
            [jnp.concatenate(highs, axis=1), jnp.concatenate(lows, axis=1)], axis=0
        )
        sums = mul(jnp.concatenate(values, axis=0), weights)
        for member in range(2):
            head = 2 * number + member
            columns = slice(member * TOK, (member + 1) * TOK)
            result = (
                sums[128 * member : 128 * member + 64, columns]
                + sums[128 * member + 64 : 128 * member + 128, columns]
            )
            parts_out[head, :HEAD_DIM] = result[:HEAD_DIM]
            parts_out[head, HEAD_DIM:] = jnp.where(
                tail_row == 1, tops[member], result[HEAD_DIM:MSG_ROWS]
            )

    def pair_copy(place):
        return pltpu.make_async_remote_copy(
            src_ref=parts_out.at[8 * (1 - col_x) + place],
            dst_ref=parts_pair.at[place],
            send_sem=pair_send.at[place],
            recv_sem=pair_recv.at[place],
            device_id=partner,
            device_id_type=MESH,
        )

    def part_copy(place, source):
        return pltpu.make_async_remote_copy(
            src_ref=parts_out.at[8 * col_x + place],
            dst_ref=parts_in.at[source],
            send_sem=part_send.at[place],
            recv_sem=part_recv.at[source],
            device_id=(row, 2 * place + col_x, seed),
            device_id_type=MESH,
        )

    places = [lax.rem(col_y + step, Y) for step in YS] + [col_y]
    twos = [lax.rem(col_y // 2 + step, 4) for step in (2, 1, 3, 0)]
    keys_values(1 - col_x)
    for two in twos:
        two_heads(1 - col_x, two)
        for member in range(2):
            pair_copy(2 * two + member).start()
    keys_values(col_x)
    for two in twos:
        two_heads(col_x, two)

    def merged(place):
        head = 8 * col_x + place
        pair_copy(place).wait_recv()
        mine, theirs = parts_out[head], parts_pair[place]
        top_mine = mine[HEAD_DIM + 1 : HEAD_DIM + 2]
        top_theirs = theirs[HEAD_DIM + 1 : HEAD_DIM + 2]
        top = jnp.maximum(top_mine, top_theirs)
        both = mine * jnp.exp(top_mine - top) + theirs * jnp.exp(top_theirs - top)
        tail = jnp.where(tail_row == 1, top, both[HEAD_DIM:])
        return both[:HEAD_DIM], tail

    for place in places[:-1]:
        head = 8 * col_x + place
        sums, tail = merged(place)
        parts_out[head, :HEAD_DIM] = sums
        parts_out[head, HEAD_DIM:] = tail
        part_copy(place, col_y).start()
    sums, tail = merged(col_y)
    parts_in[col_y, :HEAD_DIM] = sums
    parts_in[col_y, HEAD_DIM:] = tail
    for place in places[-2::-1]:
        part_copy(place, place).wait_recv()
    for place in places:
        pair_copy(place).wait_send()
    for place in places[:-1]:
        part_copy(place, col_y).wait_send()
    tops = parts_in[:, HEAD_DIM + 1 : HEAD_DIM + 2, :]
    factors = jnp.exp(tops - jnp.max(tops, axis=0, keepdims=True))
    total = jnp.sum(factors * parts_in[:, HEAD_DIM : HEAD_DIM + 1, :], axis=0)
    weighted = jnp.sum(factors * parts_in[:, :HEAD_DIM, :], axis=0)
    own = 8 * col_x + col_y
    attended[pl.ds(own, 1)] = (weighted / total)[None]

    def att_copy(place):
        return pltpu.make_async_remote_copy(
            src_ref=attended.at[own],
            dst_ref=attended.at[own],
            send_sem=att_send.at[place],
            recv_sem=att_recv.at[own],
            device_id=(row, 2 * place + col_x, seed),
            device_id_type=MESH,
        )

    def across_copy(head):
        return pltpu.make_async_remote_copy(
            src_ref=attended.at[head],
            dst_ref=attended.at[head],
            send_sem=across_send.at[lax.rem(head, 8)],
            recv_sem=att_recv.at[head],
            device_id=partner,
            device_id_type=MESH,
        )

    across_copy(own).start()
    for place in places[-2::-1]:
        att_copy(place).start()
    loads[13].wait()
    for place in places[-2::-1]:
        head = 8 * col_x + place
        across_copy(head).wait_recv()
        across_copy(head).start()

    def projected(half):
        rows = pl.ds(pl.multiple_of(half * 384, 128), 384)
        results = attended[pl.ds(8 * half, 8)].reshape(384, TOK).T
        gated_both = stacked(gates[:, rows] * results)
        terms = []
        for step in range(D // 256):
            high, low = split(out_w[rows, step * 256 : (step + 1) * 256])
            terms.append(dot_split(gated_both, high, low))
        return terms

    for step, term in enumerate(projected(col_x)):
        ada[:, step * 256 : (step + 1) * 256] = term
    for place in places[::-1]:
        across_copy(8 * (1 - col_x) + place).wait_recv()
    stores = []
    for step, term in enumerate(projected(1 - col_x)):
        columns = slice(step * 256, (step + 1) * 256)
        result[:, columns] = tokens[:, columns] + out_gate[:, columns] * (
            term + ada[:, columns]
        )
        store = pltpu.make_async_copy(
            result.at[:, columns], out_hbm.at[:, columns], store_sems.at[step]
        )
        store.start()
        stores.append(store)

    for place in places[:-1]:
        att_copy(place).wait_send()
    for place in places:
        across_copy(8 * col_x + place).wait_send()
    for store in stores:
        store.wait()


def body(
    tokens_act,
    single_cond,
    noise_level,
    fourier_freq,
    fourier_phase,
    noise_weight,
    ada_weight,
    query_gate_weight,
    kv_weight,
    out_weight,
    out_gate_weight,
    pair_bias,
    relpos_table,
    chain_id,
    residue_index,
):
    hbm = pl.BlockSpec(memory_space=pltpu.HBM)
    vmem = pltpu.VMEM
    dma = pltpu.SemaphoreType.DMA
    return pl.pallas_call(
        kernel,
        name="attention_block",
        out_shape=jax.ShapeDtypeStruct((TOK, D), F32),
        in_specs=[hbm, hbm, pl.BlockSpec(memory_space=pltpu.SMEM)] + [hbm] * 12,
        out_specs=hbm,
        scratch_shapes=[
            vmem((TOK, D), F32),
            vmem((TOK, C_S), F32),
            vmem((2, 128), F32),
            vmem((2, 128), F32),
            vmem((256, C_S), F32),
            vmem((C_S, 2 * D), F32),
            vmem((D, 2 * D), F32),
            vmem((D, 2 * D), F32),
            vmem((D, D), F32),
            vmem((C_S, D), F32),
            vmem((HEADS, TOK, TOK), BF16),
            vmem((HEADS, 2 * REL + 2), F32),
            vmem((N_ROW, TOK), jnp.int32),
            vmem((N_ROW, TOK), jnp.int32),
            vmem((TOK, 2 * D), F32),
            vmem((2, PIECES, PIECE_ROWS, D), F32),
            vmem((2, PIECES, PIECE_ROWS, D), F32),
            vmem((HEADS // 2, 256, 2 * TOK), BF16),
            vmem((HEADS // 2, 256, 2 * TOK), BF16),
            vmem((TOK, D), F32),
            vmem((TOK, D), F32),
            vmem((D, TOK), F32),
            vmem((D, TOK), F32),
            vmem((TOK, D), BF16),
            vmem((TOK, D), BF16),
            vmem((D, 2 * D), BF16),
            vmem((D, 2 * D), BF16),
            vmem((HEADS, TOK, TOK), F32),
            vmem((HEADS, MSG_ROWS, TOK), F32),
            vmem((Y, MSG_ROWS, TOK), F32),
            vmem((Y, MSG_ROWS, TOK), F32),
            vmem((HEADS, HEAD_DIM, TOK), F32),
            vmem((TOK, D), F32),
            dma((14,)),
            dma((3,)),
            dma((4, 2, PIECES)),
            dma((2, PIECES)),
            dma((2, PIECES)),
            dma((2, PIECES)),
            dma((Y,)),
            dma((Y,)),
            dma((Y,)),
            dma((Y,)),
            dma((Y,)),
            dma((Y,)),
            dma((N_COL,)),
        ],
        compiler_params=pltpu.CompilerParams(
            collective_id=0, has_side_effects=True, vmem_limit_bytes=60 * 1024 * 1024
        ),
    )(
        tokens_act,
        single_cond,
        noise_level.reshape(1, 1),
        fourier_freq.reshape(2, 128),
        fourier_phase.reshape(2, 128),
        noise_weight,
        ada_weight,
        query_gate_weight,
        kv_weight,
        out_weight,
        out_gate_weight,
        pair_bias,
        relpos_table,
        chain_id.reshape(N_ROW, TOK),
        residue_index.reshape(N_ROW, TOK),
    )


def solution(mesh):
    in_specs = (
        P(("seed", "row"), None),
        P(("seed", "row"), None),
        P("seed"),
        P(),
        P(),
        P(),
        P(),
        P(),
        P(),
        P(),
        P(),
        P(None, "row", "col"),
        P(),
        P(),
        P(),
    )
    out_specs = P(("seed", "row"), None)
    return jax.shard_map(body, mesh=mesh, in_specs=in_specs, out_specs=out_specs, check_vma=False)
```
